256 devices in a mesh: seq: 64 (over y, z, core), tp: 4 (over x).
Axes of the slice: x: 4, y: 4, z: 8, core: 2. Of those that a mesh axis runs over, the one named last changes fastest.
Arguments:
- queries: bfloat16 [8192, 4096], P('seq', 'tp'), may hold values from -10 to 10
- key_vectors: bfloat16 [8192, 512], P('seq', 'tp'), may hold values from -8.5 to 8.5
- value_vectors: bfloat16 [8192, 512], P('seq', 'tp'), may hold values from -6 to 6
- vertical: int32 [32, 16], P('tp'), may hold values from 0 to 63
- vertical_count: int32 [32], P('tp'), may hold values from 1 to 16, as said below
- slash_offsets: int32 [32, 8], P('tp'), may hold values from 1 to 63
- out_weight: bfloat16 [4096, 5120], P('tp'), may hold values from -0.09375 to 0.09375
Outputs:
- output: bfloat16 [8192, 5120], P(('seq', 'tp'))
The draws below stay inside these ranges and needn't reach their ends.
Inputs may be any that keep to these rules, and one draw needn't show every extreme that they name: `vertical_count`: a power of two for each head; 16 for some head in every draw.
All inputs are finite; a program needn't handle non-finite values.
Results may differ from the reference program's by a relative error of at most 0.019.
Values may be sent and summed in bfloat16 or wider, within the bound.
A program may use at most 128 MiB of HBM per device.

```python
import math
import jax
import jax.numpy as jnp
from jax import lax

D = 5120
QHEADS = 32
KVHEADS = 4
HEAD = 128
BLOCK = 128
NSLASH = 8
NVERT = 16
LENGTH = 8192
NB = 64


def draw_queries(key, part):
    key = jax.random.fold_in(key, 2)
    values_now = jax.random.normal(key, (LENGTH, QHEADS * HEAD), jnp.float32)
    return jnp.clip(values_now, -6.0, 6.0).astype(jnp.bfloat16)


def draw_key_vectors(key, part):
    key = jax.random.fold_in(key, 1)
    values_now = jax.random.normal(key, (LENGTH, KVHEADS * HEAD), jnp.float32)
    return jnp.clip(values_now, -6.0, 6.0).astype(jnp.bfloat16)


def draw_vertical_count(key, part):
    key = jax.random.fold_in(key, 5)
    power_key, pick_key = jax.random.split(key)
    levels = int(math.log2(NVERT)) + 1
    powers = jax.random.randint(power_key, (QHEADS,), 0, levels, dtype=jnp.int32)
    counts_now = jnp.left_shift(jnp.ones((QHEADS,), jnp.int32), powers)
    chosen_head = jax.random.randint(pick_key, (), 0, QHEADS, dtype=jnp.int32)
    head_ids = jnp.arange(QHEADS, dtype=jnp.int32)
    return jnp.where(head_ids == chosen_head, NVERT, counts_now).astype(jnp.int32)


def with_ends(result, stream_key, least, high):
    longest = result.shape.index(max(result.shape))
    spots = []
    for shift in (0, 1):
        where = [jax.random.randint(jax.random.fold_in(stream_key, axis), (), 0, length) for axis, length in enumerate(result.shape)]
        where[longest] = (where[longest] + shift) % result.shape[longest]
        spots.append(tuple(where))
    return result.at[spots[0]].set(least).at[spots[1]].set(high)


def block_scale(own_key, extent, shards, smallest, high):
    def one(axis_at, parts):
        steps = jax.random.uniform(jax.random.fold_in(jax.random.fold_in(own_key, 6), axis_at), (parts,), jnp.float32, smallest / len(shards), high / len(shards))
        return jnp.repeat(jnp.exp(steps), extent[axis_at] // parts).reshape((-1,) + (1,) * (len(extent) - axis_at - 1))

    loudness = one(*shards[0])
    for cut in shards[1:]:
        loudness = loudness * one(*cut)
    return loudness


def bell_draw(rng, dims, deviation, limit, cuts=(), kind=jnp.bfloat16):
    values = deviation * jax.random.normal(rng, dims, jnp.float32)
    if cuts:
        values = values * block_scale(rng, dims, cuts, -0.22, 0.18)
    return jnp.clip(values, -limit, limit).astype(kind)


def setup_inputs(seed: int = 0) -> dict:
    streams_of = jax.random.split(jax.random.key(seed), 8)
    queries = draw_queries(jax.random.fold_in(streams_of[7], 71), 0)
    key_vectors = draw_key_vectors(jax.random.fold_in(streams_of[7], 71), 0)
    value_vectors = bell_draw(streams_of[2], (LENGTH, KVHEADS * HEAD), 1.0, 6.0, ((0, 64), (1, 4)))
    vertical = with_ends(jax.random.randint(streams_of[3], (QHEADS, NVERT), 0, NB), jax.random.fold_in(streams_of[3], 1), 0, NB - 1).astype(jnp.int32)
    vertical_count = draw_vertical_count(jax.random.fold_in(streams_of[7], 71), 0)
    slash_offsets = with_ends(jax.random.randint(streams_of[5], (QHEADS, NSLASH), 1, NB), jax.random.fold_in(streams_of[5], 1), 1, NB - 1).astype(jnp.int32)
    out_weight = bell_draw(streams_of[6], (QHEADS * HEAD, D), (QHEADS * HEAD) ** -0.5, 0.09375, ((0, 4),))
    return dict(queries=queries, key_vectors=key_vectors, value_vectors=value_vectors, vertical=vertical, vertical_count=vertical_count, slash_offsets=slash_offsets, out_weight=out_weight)


def candidates(query_block, vert_row, allowed_count, slash_row):
    query_col = query_block[:, None]
    shifted = query_col - slash_row[None, :]
    upright = jnp.broadcast_to(vert_row[None, :], (query_block.shape[0], vert_row.shape[0]))
    listed = jnp.concatenate([query_col, shifted, upright], axis=1)
    slot_ids = jnp.arange(vert_row.shape[0], dtype=jnp.int32)
    usable = jnp.concatenate([query_col >= 0, shifted >= 0, (upright <= query_col) & (slot_ids < allowed_count)[None, :]], axis=1)
    order_ids = jnp.arange(listed.shape[1], dtype=jnp.int32)
    before = order_ids[:, None] > order_ids[None, :]
    same = listed[:, :, None] == listed[:, None, :]
    repeated = jnp.any(same & before[None, :, :] & usable[:, None, :], axis=2)
    return listed, usable & jnp.logical_not(repeated)


def reference(queries, key_vectors, value_vectors, vertical, vertical_count, slash_offsets, out_weight):
    length = queries.shape[0]
    block_count = length // BLOCK
    group_size = QHEADS // KVHEADS
    score_scale = HEAD ** -0.5
    query_blocks = queries.reshape(block_count, BLOCK, QHEADS, HEAD)
    key_blocks = key_vectors.reshape(block_count, BLOCK, KVHEADS, HEAD)
    value_blocks = value_vectors.reshape(block_count, BLOCK, KVHEADS, HEAD)
    block_ids = jnp.arange(block_count, dtype=jnp.int32)
    offsets = jnp.arange(BLOCK, dtype=jnp.int32)
    query_pos = block_ids[:, None] * BLOCK + offsets[None, :]

    def one_head(head_id):
        kv_head = head_id // group_size
        query_head = lax.dynamic_index_in_dim(query_blocks, head_id, 2, keepdims=False).astype(jnp.float32)
        key_head = lax.dynamic_index_in_dim(key_blocks, kv_head, 2, keepdims=False)
        value_head = lax.dynamic_index_in_dim(value_blocks, kv_head, 2, keepdims=False)
        listed, kept_blocks = candidates(block_ids, vertical[head_id], vertical_count[head_id], slash_offsets[head_id])
        safe_ids = jnp.clip(listed, 0, block_count - 1).astype(jnp.int32)
        key_chosen = key_head[safe_ids].astype(jnp.float32)
        value_chosen = value_head[safe_ids].astype(jnp.float32)
        scores = jnp.einsum("iqd,ickd->iqck", query_head, key_chosen, precision=lax.Precision.HIGHEST) * score_scale
        key_pos = safe_ids[:, None, :, None] * BLOCK + offsets[None, None, None, :]
        allowed = kept_blocks[:, None, :, None] & (key_pos <= query_pos[:, :, None, None])
        scores = jnp.where(allowed, scores, -jnp.inf)
        row_max = jnp.max(scores, axis=(2, 3), keepdims=True)
        exp_scores = jnp.exp(scores - row_max)
        row_sum = jnp.sum(exp_scores, axis=(2, 3), keepdims=True)
        weights = (exp_scores / row_sum).astype(jnp.bfloat16)
        attended = jnp.einsum("iqck,ickd->iqd", weights.astype(jnp.float32), value_chosen, precision=lax.Precision.HIGHEST)
        return attended.astype(jnp.bfloat16)

    attended = lax.map(one_head, jnp.arange(QHEADS, dtype=jnp.int32))
    attended = jnp.transpose(attended, (1, 2, 0, 3)).reshape(length, QHEADS * HEAD)
    return jnp.dot(attended, out_weight, preferred_element_type=jnp.float32).astype(jnp.bfloat16)
```

```python
import functools
import math

import jax
import jax.numpy as jnp
from jax import lax
from jax.experimental import pallas as pl
from jax.experimental.pallas import tpu as pltpu
from jax.sharding import PartitionSpec as P

HEAD = 128
BLOCK = 128
HEADS = 8
NY, NZ = 4, 8
NB = 64
HALF = NB // 2
NSLASH, NVERT = 8, 16
SLOTS = 1 + NSLASH + NVERT
D = 5120
PIECE = 512
SIDE = D // PIECE // 2
PIECES = 2 * SIDE
ROWS = 32
FEATURES = HEADS * HEAD
EXP2_SCALE = HEAD**-0.5 * math.log2(math.e)
MESH = pl.DeviceIdType.MESH
NEG = float("-inf")


def key_slot(core, y, z):
    return core * HALF + z * NY + y


def value_slot(core, y, z):
    return NB + core * HALF + y * NZ + z


def choose_blocks(head, me, vert_ref, count_ref, slash_ref, key_at, value_at, bias_at):
    low = jnp.where(me < 32, jnp.left_shift(jnp.int32(1), me % 32), 0)
    high = jnp.where(me < 32, 0, jnp.left_shift(jnp.int32(1), me % 32))
    count = count_ref[head]
    for c in range(1, SLOTS):
        if c <= NSLASH:
            block = me - slash_ref[head, c - 1]
            usable = block >= 0
        else:
            block = vert_ref[head, c - 1 - NSLASH]
            usable = (block <= me) & (c - 1 - NSLASH < count)
        block = jnp.clip(block, 0, NB - 1)
        bit = jnp.left_shift(jnp.int32(1), block % 32)
        in_low = block < 32
        seen = (jnp.where(in_low, low, high) & bit) != 0
        kept = usable & jnp.logical_not(seen)
        add = jnp.where(kept, bit, 0)
        low = low | jnp.where(in_low, add, 0)
        high = high | jnp.where(in_low, 0, add)
        core, z, y = block % 2, (block // 2) % NZ, block // (2 * NZ)
        key_at[head, c] = key_slot(core, y, z)
        value_at[head, c] = value_slot(core, y, z)
        bias_at[head, c] = jnp.where(kept, jnp.float32(0), jnp.float32(NEG))


def attend_head(head, q_vm, kv, key_at, value_at, bias_at, own_key, own_value, scores, att):
    query = q_vm[head]
    rows = lax.broadcasted_iota(jnp.int32, (BLOCK, BLOCK), 0)
    cols = lax.broadcasted_iota(jnp.int32, (BLOCK, BLOCK), 1)
    top = None
    for c in range(0, SLOTS, 2):
        slots = [c] if c + 1 == SLOTS else [c, c + 1]
        keys = [kv[own_key if s == 0 else key_at[head, s]] for s in slots]
        keys = keys[0] if len(keys) == 1 else jnp.concatenate(keys, axis=0)
        both = lax.dot_general(
            query, keys, (((1,), (1,)), ((), ())), preferred_element_type=jnp.float32
        )
        for n, s in enumerate(slots):
            part = both[:, n * BLOCK : (n + 1) * BLOCK]
            if s == 0:
                part = jnp.where(cols <= rows, part, NEG)
            else:
                part = part + bias_at[head, s]
            scores[:, s * BLOCK : (s + 1) * BLOCK] = part
            top = part if top is None else jnp.maximum(top, part)
    top = jnp.max(top, axis=1, keepdims=True)
    total, out = None, None
    for c in range(0, SLOTS, 2):
        slots = [c] if c + 1 == SLOTS else [c, c + 1]
        values = [kv[own_value if s == 0 else value_at[head, s]] for s in slots]
        values = values[0] if len(values) == 1 else jnp.concatenate(values, axis=0)
        wide = len(slots) * BLOCK
        weights = jnp.exp2((scores[:, c * BLOCK : c * BLOCK + wide] - top) * EXP2_SCALE)
        for n in range(len(slots)):
            part = weights[:, n * BLOCK : (n + 1) * BLOCK]
            total = part if total is None else total + part
        term = jnp.dot(weights.astype(jnp.bfloat16), values, preferred_element_type=jnp.float32)
        out = term if out is None else out + term
    out = out / jnp.sum(total, axis=1, keepdims=True)
    att[:, pl.ds(pl.multiple_of(head * HEAD, HEAD), HEAD)] = out.astype(jnp.bfloat16)


def remote(src, dst, send, recv, where):
    return pltpu.make_async_remote_copy(
        src_ref=src, dst_ref=dst, send_sem=send, recv_sem=recv, device_id=where, device_id_type=MESH
    )


def gather(k_hbm, v_hbm, kv, sems, core, y, z, up_y, down_y, up_z, down_z, twin, between):
    full_sem, half_sem, send_sem, twin_send, twin_recv, own_sem = sems

    def at_key(dy, dz):
        return key_slot(core, (y + dy + NY) % NY, (z + dz + NZ) % NZ)

    def at_value(dy, dz):
        return value_slot(core, (y + dy + NY) % NY, (z + dz + NZ) % NZ)

    def sem_of(slot):
        return slot % HALF + (slot // NB) * HALF

    def send(slot, where, half=None, source=None):
        source = kv.at[slot] if source is None else source
        target = kv.at[slot]
        if half is not None:
            source = source.at[pl.ds(half * 64, 64)]
            target = target.at[pl.ds(half * 64, 64)]
        recv = half_sem.at[sem_of(slot)] if half == 1 else full_sem.at[sem_of(slot)]
        remote(source, target, send_sem, recv, where).start()


    def pass_twin(slot, kind, source=None):
        source = kv.at[slot] if source is None else source
        remote(source, kv.at[slot], twin_send.at[kind], twin_recv.at[kind], twin).start()

    def arrived(slot, halves=False):
        if halves:
            for half, sem in ((0, full_sem), (1, half_sem)):
                piece = kv.at[slot].at[pl.ds(half * 64, 64)]
                pltpu.make_async_copy(piece, piece, sem.at[sem_of(slot)]).wait()
        else:
            pltpu.make_async_copy(kv.at[slot], kv.at[slot], full_sem.at[sem_of(slot)]).wait()

    mine_k, mine_v = at_key(0, 0), at_value(0, 0)
    for where in (up_z, down_z, up_y, down_y):
        send(mine_v, where, source=v_hbm)
        send(mine_k, where, source=k_hbm)
    pass_twin(mine_k, 0, k_hbm)
    pass_twin(mine_v, 1, v_hbm)
    between()

    events = []

    def key_column(dy):
        slot = at_key(dy, 0)
        send(slot, up_z)
        send(slot, down_z)
        pass_twin(slot, 0)

    def key_y_near():
        arrived(at_key(-1, 0))
        send(at_key(-1, 0), up_y, half=0)
        key_column(-1)
        arrived(at_key(1, 0))
        send(at_key(1, 0), down_y, half=1)
        key_column(1)

    def key_y_far():
        arrived(at_key(2, 0), halves=True)
        key_column(2)

    def key_z(dy, dz):
        for sign, where in ((-1, up_z), (1, down_z)):
            slot = at_key(dy, sign * dz)
            if dz == 4 and sign == 1:
                continue
            arrived(slot)
            if dz < 3 or (dz == 3 and (dy in (0, -1)) == (sign == -1)):
                send(slot, where)
            pass_twin(slot, 0)

    def value_row(dz):
        slot = at_value(0, dz)
        send(slot, up_y)
        send(slot, down_y)
        pass_twin(slot, 1)

    def value_z(dz):
        if dz == 4:
            arrived(at_value(0, 4), halves=True)
            value_row(4)
            return
        for sign, where, half in ((-1, up_z, 0), (1, down_z, 1)):
            slot = at_value(0, sign * dz)
            arrived(slot)
            if dz < 3:
                send(slot, where)
            else:
                send(slot, where, half=half)
            value_row(sign * dz)

    def value_y_near(dz):
        for sign, where in ((-1, up_y), (1, down_y)):
            slot = at_value(sign, dz)
            arrived(slot)
            if (dz <= 0) == (sign == -1):
                send(slot, where)
            pass_twin(slot, 1)

    def value_y_far(dz):
        slot = at_value(2, dz)
        arrived(slot)
        pass_twin(slot, 1)

    events.append((1, 0, lambda: value_z(1)))
    events.append((1, 1, key_y_near))
    events.append((2, 1, key_y_far))
    for d in (2, 3, 4):
        events.append((d, 0, lambda d=d: value_z(d)))
    for dy, base in ((0, 0), (-1, 1), (1, 1), (2, 2)):
        for d in (1, 2, 3, 4):
            events.append((base + d, 2, lambda dy=dy, d=d: key_z(dy, d)))
    for dz in (0, -1, 1, -2, 2, -3, 3, 4):
        events.append((abs(dz) + 1, 3, lambda dz=dz: value_y_near(dz)))
        events.append((abs(dz) + 2, 4, lambda dz=dz: value_y_far(dz)))
    for _, _, handler in sorted(events, key=lambda e: e[:2]):
        handler()

    other = (1 - core) * HALF
    for kind, base in ((0, 0), (1, NB)):
        half = kv.at[pl.ds(base + other, HALF)]
        pltpu.make_async_copy(half, half, twin_recv.at[kind]).wait()
        pltpu.make_async_copy(half, half, twin_send.at[kind]).wait()
    sent = kv.at[pl.ds(0, 62)]
    pltpu.make_async_copy(sent, sent, send_sem).wait()


def kernel(
    vert_ref, count_ref, slash_ref, q_hbm, k_hbm, v_hbm, w_hbm, out_ref,
    kv, q_vm, w_vm, scores, att, part, opp_in, dir_in, sum_in, sum_out,
    key_at, value_at, bias_at,
    full_sem, half_sem, send_sem, twin_send, twin_recv, own_sem, q_sem, w_sem,
    opp_sem, dir_sem, sum_sem, first_send, second_send,
):
    me, tp = lax.axis_index("seq"), lax.axis_index("tp")
    core, z, y = me % 2, (me // 2) % NZ, me // (2 * NZ)

    def seq_at(core, y, z):
        return {"seq": ((y + NY) % NY * NZ + (z + NZ) % NZ) * 2 + core}

    up_y, down_y = seq_at(core, y + 1, z), seq_at(core, y - 1, z)
    up_z, down_z = seq_at(core, y, z + 1), seq_at(core, y, z - 1)
    twin = seq_at(1 - core, y, z)
    right, left = {"tp": (tp + 1) % 4}, {"tp": (tp + 3) % 4}

    own_key, own_value = key_slot(core, y, z), value_slot(core, y, z)
    own_copies = [
        pltpu.make_async_copy(k_hbm, kv.at[own_key], own_sem.at[0]),
        pltpu.make_async_copy(v_hbm, kv.at[own_value], own_sem.at[1]),
    ]
    for copy in own_copies:
        copy.start()

    barrier = pltpu.get_barrier_semaphore()
    neighbours = (up_y, down_y, up_z, down_z, twin, right, left)
    for where in neighbours:
        pl.semaphore_signal(barrier, inc=1, device_id=where, device_id_type=MESH)
    pl.semaphore_wait(barrier, len(neighbours))

    def between():
        for head in range(HEADS):
            pltpu.make_async_copy(
                q_hbm.at[:, pl.ds(head * HEAD, HEAD)], q_vm.at[head], q_sem
            ).start()
        for p in range(PIECES):
            pltpu.make_async_copy(
                w_hbm.at[:, pl.ds(p * PIECE, PIECE)], w_vm.at[p], w_sem.at[p]
            ).start()

        @pl.loop(0, HEADS)
        def _(head):
            choose_blocks(head, me, vert_ref, count_ref, slash_ref, key_at, value_at, bias_at)

    gather(
        k_hbm, v_hbm, kv,
        (full_sem, half_sem, send_sem, twin_send, twin_recv, own_sem),
        core, y, z, up_y, down_y, up_z, down_z, twin, between,
    )
    for copy in own_copies:
        copy.wait()
    pltpu.make_async_copy(q_vm, q_vm, q_sem).wait()

    @pl.loop(0, HEADS // 2)
    def _(pair):
        for n in range(2):
            attend_head(
                pair * 2 + n, q_vm, kv, key_at, value_at, bias_at,
                own_key, own_value, scores.at[n], att,
            )

    def rows_of(p, target):
        return part.at[p, pl.ds(pl.multiple_of((target + 4) % 4 * ROWS, ROWS), ROWS)]

    @pl.loop(0, SIDE)
    def _(j):
        for p, ahead, behind, step in ((j, right, left, 1), (j + SIDE, left, right, -1)):
            pltpu.make_async_copy(w_vm.at[p], w_vm.at[p], w_sem.at[p]).wait()
            part[p] = jnp.dot(att[...], w_vm[p], preferred_element_type=jnp.float32).astype(
                jnp.bfloat16
            )
            remote(rows_of(p, tp + 2), opp_in.at[p], first_send, opp_sem.at[p], ahead).start()
            remote(rows_of(p, tp - step), dir_in.at[p], first_send, dir_sem.at[p], behind).start()

    @pl.loop(0, SIDE)
    def _(j):
        for p, ahead, step in ((j, right, 1), (j + SIDE, left, -1)):
            pltpu.make_async_copy(opp_in.at[p], opp_in.at[p], opp_sem.at[p]).wait()
            summed = opp_in[p].astype(jnp.float32) + rows_of(p, tp + step)[...].astype(jnp.float32)
            sum_out[p] = summed.astype(jnp.bfloat16)
            remote(sum_out.at[p], sum_in.at[p], second_send, sum_sem.at[p], ahead).start()

    for j in range(SIDE):
        for p in (j, j + SIDE):
            pltpu.make_async_copy(dir_in.at[p], dir_in.at[p], dir_sem.at[p]).wait()
            pltpu.make_async_copy(sum_in.at[p], sum_in.at[p], sum_sem.at[p]).wait()
            whole = (
                rows_of(p, tp)[...].astype(jnp.float32)
                + dir_in[p].astype(jnp.float32)
                + sum_in[p].astype(jnp.float32)
            )
            out_ref[:, p * PIECE : (p + 1) * PIECE] = whole.astype(jnp.bfloat16)
    pltpu.make_async_copy(part.at[pl.ds(0, SIDE)], part.at[pl.ds(0, SIDE)], first_send).wait()
    pltpu.make_async_copy(sum_out, sum_out, second_send).wait()


def body(queries, key_vectors, value_vectors, vertical, vertical_count, slash_offsets, out_weight):
    smem = pl.BlockSpec(memory_space=pltpu.SMEM)
    anywhere = pl.BlockSpec(memory_space=pl.ANY)
    bf16, dma = jnp.bfloat16, pltpu.SemaphoreType.DMA
    return pl.pallas_call(
        kernel,
        out_shape=jax.ShapeDtypeStruct((ROWS, D), bf16),
        in_specs=[smem] * 3 + [anywhere] * 4,
        out_specs=pl.BlockSpec(memory_space=pltpu.VMEM),
        scratch_shapes=[
            pltpu.VMEM((2 * NB, BLOCK, HEAD), bf16),
            pltpu.VMEM((HEADS, BLOCK, HEAD), bf16),
            pltpu.VMEM((PIECES, FEATURES, PIECE), bf16),
            pltpu.VMEM((2, BLOCK, SLOTS * BLOCK), jnp.float32),
            pltpu.VMEM((BLOCK, FEATURES), bf16),
            pltpu.VMEM((PIECES, BLOCK, PIECE), bf16),
            pltpu.VMEM((PIECES, ROWS, PIECE), bf16),
            pltpu.VMEM((PIECES, ROWS, PIECE), bf16),
            pltpu.VMEM((PIECES, ROWS, PIECE), bf16),
            pltpu.VMEM((PIECES, ROWS, PIECE), bf16),
            pltpu.SMEM((HEADS, 32), jnp.int32),
            pltpu.SMEM((HEADS, 32), jnp.int32),
            pltpu.SMEM((HEADS, 32), jnp.float32),
            dma((NB,)),
            dma((NB,)),
            dma,
            dma((2,)),
            dma((2,)),
            dma((2,)),
            dma,
            dma((PIECES,)),
            dma((PIECES,)),
            dma((PIECES,)),
            dma((PIECES,)),
            dma,
            dma,
        ],
        compiler_params=pltpu.CompilerParams(
            collective_id=0, has_side_effects=True, vmem_limit_bytes=48 * 1024 * 1024
        ),
        cost_estimate=pl.CostEstimate(
            flops=3_200_000_000, bytes_accessed=16_000_000, transcendentals=3_300_000
        ),
        name="attend_project",
    )(vertical, vertical_count, slash_offsets, queries, key_vectors, value_vectors, out_weight)


def solution(mesh):
    in_specs = (
        P("seq", "tp"),
        P("seq", "tp"),
        P("seq", "tp"),
        P("tp", None),
        P("tp"),
        P("tp", None),
        P("tp", None),
    )
    out_specs = P(("seq", "tp"), None)
    return jax.shard_map(body, mesh=mesh, in_specs=in_specs, out_specs=out_specs, check_vma=False)
```

```python
import functools
import math

import jax
import jax.numpy as jnp
from jax import lax
from jax.experimental import pallas as pl
from jax.experimental.pallas import tpu as pltpu
from jax.sharding import PartitionSpec as P

HEAD = 128
BLOCK = 128
HEADS = 8
NY, NZ = 4, 8
NB = 64
HALF = NB // 2
NSLASH, NVERT = 8, 16
SLOTS = 1 + NSLASH + NVERT
D = 5120
PIECE = 512
SIDE = D // PIECE // 2
PIECES = 2 * SIDE
ROWS = 32
FEATURES = HEADS * HEAD
EXP2_SCALE = HEAD**-0.5 * math.log2(math.e)
MESH = pl.DeviceIdType.MESH
NEG = float("-inf")


def key_slot(core, y, z):
    return core * HALF + z * NY + y


def value_slot(core, y, z):
    return core * HALF + y * NZ + z


def choose_blocks(head, me, vert_ref, count_ref, slash_ref, key_at, value_at, bias_at):
    low = jnp.where(me < 32, jnp.left_shift(jnp.int32(1), me % 32), 0)
    high = jnp.where(me < 32, 0, jnp.left_shift(jnp.int32(1), me % 32))
    count = count_ref[head]
    for c in range(1, SLOTS):
        if c <= NSLASH:
            block = me - slash_ref[head, c - 1]
            usable = block >= 0
        else:
            block = vert_ref[head, c - 1 - NSLASH]
            usable = (block <= me) & (c - 1 - NSLASH < count)
        block = jnp.clip(block, 0, NB - 1)
        bit = jnp.left_shift(jnp.int32(1), block % 32)
        in_low = block < 32
        seen = (jnp.where(in_low, low, high) & bit) != 0
        kept = usable & jnp.logical_not(seen)
        add = jnp.where(kept, bit, 0)
        low = low | jnp.where(in_low, add, 0)
        high = high | jnp.where(in_low, 0, add)
        core, z, y = block % 2, (block // 2) % NZ, block // (2 * NZ)
        key_at[head, c] = key_slot(core, y, z)
        value_at[head, c] = value_slot(core, y, z)
        bias_at[head, c] = jnp.where(kept, jnp.float32(0), jnp.float32(NEG))


def slot_groups(size):
    return [list(range(c, min(c + size, SLOTS))) for c in range(0, SLOTS, size)]


def weigh_head(head, q_vm, keys_vm, key_at, bias_at, own_key, scores, weights, scale_by):
    query = q_vm[head]
    rows = lax.broadcasted_iota(jnp.int32, (BLOCK, BLOCK), 0)
    cols = lax.broadcasted_iota(jnp.int32, (BLOCK, BLOCK), 1)
    top = None
    for slots in slot_groups(2):
        keys = [keys_vm[own_key if s == 0 else key_at[head, s]] for s in slots]
        keys = keys[0] if len(keys) == 1 else jnp.concatenate(keys, axis=0)
        both = lax.dot_general(
            query, keys, (((1,), (1,)), ((), ())), preferred_element_type=jnp.float32
        )
        for n, s in enumerate(slots):
            part = both[:, n * BLOCK : (n + 1) * BLOCK]
            if s == 0:
                part = jnp.where(cols <= rows, part, NEG)
            else:
                part = part + bias_at[head, s]
            scores[:, s * BLOCK : (s + 1) * BLOCK] = part
            top = part if top is None else jnp.maximum(top, part)
    top = jnp.max(top, axis=1, keepdims=True)
    total = None
    for s in range(SLOTS):
        at = slice(s * BLOCK, (s + 1) * BLOCK)
        part = jnp.exp2((scores[:, at] - top) * EXP2_SCALE)
        weights[head, :, at] = part.astype(jnp.bfloat16)
        total = part if total is None else total + part
    total = jnp.sum(total, axis=1, keepdims=True)
    scale_by[head] = jnp.broadcast_to(1.0 / total, (BLOCK, HEAD))


def combine_head(head, values_vm, value_at, own_value, weights, scale_by, att):
    out = None
    for slots in slot_groups(4):
        values = [values_vm[own_value if s == 0 else value_at[head, s]] for s in slots]
        values = values[0] if len(values) == 1 else jnp.concatenate(values, axis=0)
        part = weights[head, :, slots[0] * BLOCK : (slots[-1] + 1) * BLOCK]
        term = jnp.dot(part, values, preferred_element_type=jnp.float32)
        out = term if out is None else out + term
    out = out * scale_by[head]
    att[:, pl.ds(pl.multiple_of(head * HEAD, HEAD), HEAD)] = out.astype(jnp.bfloat16)


def remote(src, dst, send, recv, where):
    return pltpu.make_async_remote_copy(
        src_ref=src, dst_ref=dst, send_sem=send, recv_sem=recv, device_id=where, device_id_type=MESH
    )


class Gather:
    def __init__(self, buffers, sems, sources, core, y, z, seq_at):
        self.buffers, self.sources, self.core, self.y, self.z = buffers, sources, core, y, z
        self.full_sem, self.half_sem, self.send_sem, self.twin_send, self.twin_recv = sems
        self.up_y, self.down_y = seq_at(core, y + 1, z), seq_at(core, y - 1, z)
        self.far_y = seq_at(core, y + 2, z)
        self.along = {d: seq_at(core, y, z + d) for d in (-2, -1, 1, 2)}
        self.twin = seq_at(1 - core, y, z)

    def slot(self, kind, dy, dz):
        at = key_slot if kind == 0 else value_slot
        return at(self.core, (self.y + dy + NY) % NY, (self.z + dz + NZ) % NZ)

    def send(self, kind, slot, where, half=None, source=None):
        target = self.buffers[kind].at[slot]
        source = target if source is None else source
        if half is not None:
            source = source.at[pl.ds(half * 64, 64)]
            target = target.at[pl.ds(half * 64, 64)]
        recv = (self.half_sem if half == 1 else self.full_sem).at[kind, slot % HALF]
        remote(source, target, self.send_sem.at[kind], recv, where).start()

    def to_twin(self, kind, slot, source=None):
        target = self.buffers[kind].at[slot]
        source = target if source is None else source
        send, recv = self.twin_send.at[kind], self.twin_recv.at[kind]
        remote(source, target, send, recv, self.twin).start()

    def arrived(self, kind, slot, halves=False):
        whole = self.buffers[kind].at[slot]
        if halves:
            for half, sem in ((0, self.full_sem), (1, self.half_sem)):
                piece = whole.at[pl.ds(half * 64, 64)]
                pltpu.make_async_copy(piece, piece, sem.at[kind, slot % HALF]).wait()
        else:
            pltpu.make_async_copy(whole, whole, self.full_sem.at[kind, slot % HALF]).wait()

    def start(self, kind):
        source, slot = self.sources[kind], self.slot(kind, 0, 0)
        self.send(kind, slot, self.far_y, source=source)
        for d in (2, -2, 1, -1):
            self.send(kind, slot, self.along[d], source=source)
        for where in (self.up_y, self.down_y):
            self.send(kind, slot, where, source=source)
        self.to_twin(kind, slot, source)

    def sideways(self, kind, slot):
        self.send(kind, slot, self.up_y)
        self.send(kind, slot, self.down_y)

    def onward(self, kind, slot, sign):
        self.send(kind, slot, self.along[sign])
        self.send(kind, slot, self.along[2 * sign], half=0 if sign == 1 else 1)

    def near(self, kind):
        slot = self.slot(kind, 2, 0)
        self.arrived(kind, slot)
        for d in (2, -2, 1, -1):
            self.send(kind, slot, self.along[d])
        self.to_twin(kind, slot)
        for sign in (1, -1):
            slot = self.slot(kind, 0, -2 * sign)
            self.arrived(kind, slot)
            self.onward(kind, slot, sign)
            self.sideways(kind, slot)
            self.to_twin(kind, slot)
        for sign in (1, -1):
            slot = self.slot(kind, 0, -sign)
            self.arrived(kind, slot)
            self.sideways(kind, slot)
            self.to_twin(kind, slot)

    def middle(self, kind):
        for sign in (1, -1):
            slot = self.slot(kind, 0, -3 * sign)
            self.arrived(kind, slot)
            self.sideways(kind, slot)
            self.to_twin(kind, slot)
        slot = self.slot(kind, 0, 4)
        self.arrived(kind, slot, halves=True)
        self.sideways(kind, slot)
        self.to_twin(kind, slot)
        for sign in (1, -1):
            slot = self.slot(kind, 2, -2 * sign)
            self.arrived(kind, slot)
            self.onward(kind, slot, sign)
            self.to_twin(kind, slot)

    def last(self, kind):
        todo = []
        for dz in (0, 1, -1, 2, -2):
            todo += [(1, dz, False), (-1, dz, False)]
        todo += [(2, 1, False), (2, -1, False)]
        for dz in (3, -3):
            todo += [(1, dz, False), (-1, dz, False), (2, dz, False)]
        todo += [(1, 4, False), (-1, 4, False), (2, 4, True)]

        def one(dy, dz, halves):
            slot = self.slot(kind, dy, dz)
            self.arrived(kind, slot, halves)
            self.to_twin(kind, slot)

        return [functools.partial(one, *t) for t in todo]

    def other_half(self, kind):
        half = self.buffers[kind].at[pl.ds((1 - self.core) * HALF, HALF)]
        pltpu.make_async_copy(half, half, self.twin_recv.at[kind]).wait()

    def sent(self):
        for kind, buffer in enumerate(self.buffers):
            half, every = buffer.at[pl.ds(0, HALF)], buffer.at[pl.ds(0, HALF - 1)]
            pltpu.make_async_copy(half, half, self.twin_send.at[kind]).wait()
            pltpu.make_async_copy(every, every, self.send_sem.at[kind]).wait()


def kernel(
    vert_hbm, count_hbm, slash_hbm, q_hbm, k_hbm, v_hbm, w_hbm, out_hbm,
    keys_vm, values_vm, q_vm, w_vm, scores, weights, scale_by, att, part,
    opp_in, dir_in, sum_in, sum_out, out_vm,
    vert_ref, count_ref, slash_ref, key_at, value_at, bias_at,
    full_sem, half_sem, send_sem, twin_send, twin_recv, own_sem, q_sem, w_sem, out_sem,
    opp_sem, dir_sem, sum_sem, first_send, second_send,
):
    me, tp = lax.axis_index("seq"), lax.axis_index("tp")
    core, z, y = me % 2, (me // 2) % NZ, me // (2 * NZ)

    def seq_at(core, y, z):
        return {"seq": ((y + NY) % NY * NZ + (z + NZ) % NZ) * 2 + core}

    right, left = {"tp": (tp + 1) % 4}, {"tp": (tp + 3) % 4}
    own_key, own_value = key_slot(core, y, z), value_slot(core, y, z)
    own_copies = [
        pltpu.make_async_copy(source, target, own_sem.at[n])
        for n, (source, target) in enumerate(
            (
                (k_hbm, keys_vm.at[own_key]),
                (v_hbm, values_vm.at[own_value]),
                (vert_hbm, vert_ref),
                (count_hbm, count_ref),
                (slash_hbm, slash_ref),
            )
        )
    ]
    for copy in own_copies:
        copy.start()
    for head in range(HEADS):
        pltpu.make_async_copy(
            q_hbm.at[:, pl.ds(head * HEAD, HEAD)], q_vm.at[head], q_sem
        ).start()
    for p in range(PIECES):
        pltpu.make_async_copy(
            w_hbm.at[:, pl.ds(p * PIECE, PIECE)], w_vm.at[p], w_sem.at[p]
        ).start()

    moves = Gather(
        (keys_vm, values_vm), (full_sem, half_sem, send_sem, twin_send, twin_recv),
        (k_hbm, v_hbm), core, y, z, seq_at,
    )
    barrier = pltpu.get_barrier_semaphore()
    neighbours = (
        moves.up_y, moves.down_y, moves.far_y, moves.twin, right, left, *moves.along.values()
    )
    for where in neighbours:
        pl.semaphore_signal(barrier, inc=1, device_id=where, device_id_type=MESH)
    pl.semaphore_wait(barrier, len(neighbours))

    moves.start(0)
    moves.start(1)
    for copy in own_copies:
        copy.wait()

    @pl.loop(0, HEADS)
    def _(head):
        choose_blocks(head, me, vert_ref, count_ref, slash_ref, key_at, value_at, bias_at)

    moves.near(0)
    moves.near(1)
    moves.middle(0)
    moves.middle(1)
    for handler in moves.last(0):
        handler()
    pltpu.make_async_copy(q_vm, q_vm, q_sem).wait()
    moves.other_half(0)

    def weigh(head, n):
        weigh_head(
            head, q_vm, keys_vm, key_at, bias_at, own_key, scores.at[n], weights, scale_by
        )

    @pl.loop(0, HEADS // 4)
    def _(pair):
        weigh(pair * 2, 0)
        weigh(pair * 2 + 1, 1)

    handlers = moves.last(1)
    half_way = len(handlers) // 2
    for handler in handlers[:half_way]:
        handler()
    weigh(HEADS // 2, 0)
    weigh(HEADS // 2 + 1, 1)
    for handler in handlers[half_way:]:
        handler()
    weigh(HEADS // 2 + 2, 0)
    weigh(HEADS // 2 + 3, 1)
    moves.other_half(1)

    @pl.loop(0, HEADS // 2)
    def _(pair):
        for n in range(2):
            combine_head(pair * 2 + n, values_vm, value_at, own_value, weights, scale_by, att)

    def rows_of(p, target):
        return part.at[p, pl.ds(pl.multiple_of((target + 4) % 4 * ROWS, ROWS), ROWS)]

    @pl.loop(0, SIDE)
    def _(j):
        for p, ahead, behind, step in ((j, right, left, 1), (j + SIDE, left, right, -1)):
            pltpu.make_async_copy(w_vm.at[p], w_vm.at[p], w_sem.at[p]).wait()
            part[p] = jnp.dot(att[...], w_vm[p], preferred_element_type=jnp.float32).astype(
                jnp.bfloat16
            )
            remote(rows_of(p, tp + 2), opp_in.at[p], first_send, opp_sem.at[p], ahead).start()
            remote(rows_of(p, tp - step), dir_in.at[p], first_send, dir_sem.at[p], behind).start()

    @pl.loop(0, SIDE)
    def _(j):
        for p, ahead, step in ((j, right, 1), (j + SIDE, left, -1)):
            pltpu.make_async_copy(opp_in.at[p], opp_in.at[p], opp_sem.at[p]).wait()
            summed = opp_in[p].astype(jnp.float32) + rows_of(p, tp + step)[...].astype(jnp.float32)
            sum_out[p] = summed.astype(jnp.bfloat16)
            remote(sum_out.at[p], sum_in.at[p], second_send, sum_sem.at[p], ahead).start()

    for j in range(SIDE):
        for p in (j, j + SIDE):
            pltpu.make_async_copy(dir_in.at[p], dir_in.at[p], dir_sem.at[p]).wait()
            pltpu.make_async_copy(sum_in.at[p], sum_in.at[p], sum_sem.at[p]).wait()
            whole = (
                rows_of(p, tp)[...].astype(jnp.float32)
                + dir_in[p].astype(jnp.float32)
                + sum_in[p].astype(jnp.float32)
            )
            at = slice(p * PIECE, (p + 1) * PIECE)
            out_vm[:, at] = whole.astype(jnp.bfloat16)
            pltpu.make_async_copy(out_vm.at[:, at], out_hbm.at[:, at], out_sem).start()
    pltpu.make_async_copy(part.at[pl.ds(0, SIDE)], part.at[pl.ds(0, SIDE)], first_send).wait()
    pltpu.make_async_copy(sum_out, sum_out, second_send).wait()
    moves.sent()
    pltpu.make_async_copy(out_vm, out_hbm, out_sem).wait()


def body(queries, key_vectors, value_vectors, vertical, vertical_count, slash_offsets, out_weight):
    anywhere = pl.BlockSpec(memory_space=pl.ANY)
    bf16, dma = jnp.bfloat16, pltpu.SemaphoreType.DMA
    return pl.pallas_call(
        kernel,
        out_shape=jax.ShapeDtypeStruct((ROWS, D), bf16),
        in_specs=[anywhere] * 7,
        out_specs=anywhere,
        scratch_shapes=[
            pltpu.VMEM((NB, BLOCK, HEAD), bf16),
            pltpu.VMEM((NB, BLOCK, HEAD), bf16),
            pltpu.VMEM((HEADS, BLOCK, HEAD), bf16),
            pltpu.VMEM((PIECES, FEATURES, PIECE), bf16),
            pltpu.VMEM((2, BLOCK, SLOTS * BLOCK), jnp.float32),
            pltpu.VMEM((HEADS, BLOCK, SLOTS * BLOCK), bf16),
            pltpu.VMEM((HEADS, BLOCK, HEAD), jnp.float32),
            pltpu.VMEM((BLOCK, FEATURES), bf16),
            pltpu.VMEM((PIECES, BLOCK, PIECE), bf16),
            pltpu.VMEM((PIECES, ROWS, PIECE), bf16),
            pltpu.VMEM((PIECES, ROWS, PIECE), bf16),
            pltpu.VMEM((PIECES, ROWS, PIECE), bf16),
            pltpu.VMEM((PIECES, ROWS, PIECE), bf16),
            pltpu.VMEM((ROWS, D), bf16),
            pltpu.SMEM((HEADS, NVERT), jnp.int32),
            pltpu.SMEM((HEADS,), jnp.int32),
            pltpu.SMEM((HEADS, NSLASH), jnp.int32),
            pltpu.SMEM((HEADS, 32), jnp.int32),
            pltpu.SMEM((HEADS, 32), jnp.int32),
            pltpu.SMEM((HEADS, 32), jnp.float32),
            dma((2, HALF)),
            dma((2, HALF)),
            dma((2,)),
            dma((2,)),
            dma((2,)),
            dma((5,)),
            dma,
            dma((PIECES,)),
            dma,
            dma((PIECES,)),
            dma((PIECES,)),
            dma((PIECES,)),
            dma,
            dma,
        ],
        compiler_params=pltpu.CompilerParams(
            collective_id=0, has_side_effects=True, vmem_limit_bytes=64 * 1024 * 1024
        ),
        cost_estimate=pl.CostEstimate(
            flops=3_200_000_000, bytes_accessed=16_000_000, transcendentals=3_300_000
        ),
        name="attend_project",
    )(vertical, vertical_count, slash_offsets, queries, key_vectors, value_vectors, out_weight)


def solution(mesh):
    in_specs = (
        P("seq", "tp"),
        P("seq", "tp"),
        P("seq", "tp"),
        P("tp", None),
        P("tp"),
        P("tp", None),
        P("tp", None),
    )
    out_specs = P(("seq", "tp"), None)
    return jax.shard_map(body, mesh=mesh, in_specs=in_specs, out_specs=out_specs, check_vma=False)
```

```python
import functools
import math

import jax
import jax.numpy as jnp
from jax import lax
from jax.experimental import pallas as pl
from jax.experimental.pallas import tpu as pltpu
from jax.sharding import PartitionSpec as P

HEAD = 128
BLOCK = 128
HEADS = 8
NY, NZ = 4, 8
NB = 64
HALF = NB // 2
NSLASH, NVERT = 8, 16
SLOTS = 1 + NSLASH + NVERT
D = 5120
PIECE = 512
SIDE = D // PIECE // 2
PIECES = 2 * SIDE
ROWS = 32
FEATURES = HEADS * HEAD
EXP2_SCALE = HEAD**-0.5 * math.log2(math.e)
MESH = pl.DeviceIdType.MESH
CUTS = (0, 2, 4, 6)
ROW_BLOCKS = tuple(NZ * (row + 1) for row in range(NY))
SENT = (24, 16, 22, 14)
HOPS_Z = (0, 1, 1, 2, 2)
NEG = float("-inf")


def key_slot(core, y, z):
    return core * HALF + z * NY + y


def value_slot(core, y, z):
    return core * HALF + y * NZ + z


def choose_blocks(head, me, vert_ref, count_ref, slash_ref, key_at, value_at, bias_at):
    low = jnp.where(me < 32, jnp.left_shift(jnp.int32(1), me % 32), 0)
    high = jnp.where(me < 32, 0, jnp.left_shift(jnp.int32(1), me % 32))
    count = count_ref[head]
    for c in range(1, SLOTS):
        if c <= NSLASH:
            block = me - slash_ref[head, c - 1]
            usable = block >= 0
        else:
            block = vert_ref[head, c - 1 - NSLASH]
            usable = (block <= me) & (c - 1 - NSLASH < count)
        block = jnp.where(usable, block, me)
        bit = jnp.left_shift(jnp.int32(1), block % 32)
        in_low = block < 32
        seen = (jnp.where(in_low, low, high) & bit) != 0
        kept = usable & jnp.logical_not(seen)
        add = jnp.where(kept, bit, 0)
        low = low | jnp.where(in_low, add, 0)
        high = high | jnp.where(in_low, 0, add)
        core, z, y = block % 2, (block // 2) % NZ, block // (2 * NZ)
        key_at[head, c] = key_slot(core, y, z)
        value_at[head, c] = value_slot(core, y, z)
        bias_at[head, c] = jnp.where(kept, jnp.float32(0), jnp.float32(NEG))


def slot_groups(size):
    return [list(range(c, min(c + size, SLOTS))) for c in range(0, SLOTS, size)]


def weigh_head(head, q_vm, keys_vm, key_at, bias_at, own_key, scores, weights, scale_by):
    query = q_vm[head]
    rows = lax.broadcasted_iota(jnp.int32, (BLOCK, BLOCK), 0)
    cols = lax.broadcasted_iota(jnp.int32, (BLOCK, BLOCK), 1)
    top = None
    for slots in slot_groups(2):
        keys = [keys_vm[own_key if s == 0 else key_at[head, s]] for s in slots]
        keys = keys[0] if len(keys) == 1 else jnp.concatenate(keys, axis=0)
        both = lax.dot_general(
            query, keys, (((1,), (1,)), ((), ())), preferred_element_type=jnp.float32
        )
        for n, s in enumerate(slots):
            part = both[:, n * BLOCK : (n + 1) * BLOCK]
            if s == 0:
                part = jnp.where(cols <= rows, part, NEG)
            else:
                part = part + bias_at[head, s]
            scores[:, s * BLOCK : (s + 1) * BLOCK] = part
            top = part if top is None else jnp.maximum(top, part)
    top = jnp.max(top, axis=1, keepdims=True)
    total = None
    for s in range(SLOTS):
        at = slice(s * BLOCK, (s + 1) * BLOCK)
        part = jnp.exp2((scores[:, at] - top) * EXP2_SCALE)
        weights[head, :, at] = part.astype(jnp.bfloat16)
        total = part if total is None else total + part
    total = jnp.sum(total, axis=1, keepdims=True)
    scale_by[head] = jnp.broadcast_to(1.0 / total, (BLOCK, HEAD))


def combine_head(head, values_vm, value_at, own_value, weights, scale_by, att):
    out = None
    for slots in slot_groups(4):
        values = [values_vm[own_value if s == 0 else value_at[head, s]] for s in slots]
        values = values[0] if len(values) == 1 else jnp.concatenate(values, axis=0)
        part = weights[head, :, slots[0] * BLOCK : (slots[-1] + 1) * BLOCK]
        term = jnp.dot(part, values, preferred_element_type=jnp.float32)
        out = term if out is None else out + term
    out = out * scale_by[head]
    att[:, pl.ds(pl.multiple_of(head * HEAD, HEAD), HEAD)] = out.astype(jnp.bfloat16)


def remote(src, dst, send, recv, where):
    return pltpu.make_async_remote_copy(
        src_ref=src, dst_ref=dst, send_sem=send, recv_sem=recv, device_id=where, device_id_type=MESH
    )


class Gather:
    def __init__(self, buffers, sems, sources, core, y, z, seq_at):
        self.buffers, self.sources, self.core, self.y, self.z = buffers, sources, core, y, z
        self.full_sem, self.half_sem, self.send_sem, self.twin_send, self.twin_recv = sems
        other = 1 - core
        self.up_y, self.down_y = seq_at(other, y + 1, z), seq_at(other, y - 1, z)
        self.far_y = seq_at(other, y + 2, z)
        self.along = {d: seq_at(other, y, z + d) for d in (-2, -1, 1, 2)}
        self.twin = seq_at(1 - core, y, z)

    def slot(self, kind, dy, dz):
        hops = HOPS_Z[abs(dz)] + (dy in (1, -1)) if abs(dy) < 2 else 1 + HOPS_Z[abs(dz)]
        core = self.core if hops % 2 == 0 else 1 - self.core
        at = key_slot if kind == 0 else value_slot
        return at(core, (self.y + dy + NY) % NY, (self.z + dz + NZ) % NZ)

    def send(self, kind, slot, where, half=None, source=None):
        target = self.buffers[kind].at[slot]
        source = target if source is None else source
        if half is not None:
            source = source.at[pl.ds(half * 64, 64)]
            target = target.at[pl.ds(half * 64, 64)]
        recv = (self.half_sem if half == 1 else self.full_sem).at[kind, slot % HALF]
        remote(source, target, self.send_sem.at[kind], recv, where).start()

    def to_twin(self, kind, slot, source=None):
        target = self.buffers[kind].at[slot]
        source = target if source is None else source
        send, recv = self.twin_send.at[kind], self.twin_recv.at[kind]
        remote(source, target, send, recv, self.twin).start()

    def arrived(self, kind, slot, halves=False):
        whole = self.buffers[kind].at[slot]
        if halves:
            for half, sem in ((0, self.full_sem), (1, self.half_sem)):
                piece = whole.at[pl.ds(half * 64, 64)]
                pltpu.make_async_copy(piece, piece, sem.at[kind, slot % HALF]).wait()
        else:
            pltpu.make_async_copy(whole, whole, self.full_sem.at[kind, slot % HALF]).wait()

    def beside(self, kind, slot, source=None):
        @pl.when(self.y < NY - 1)
        def _():
            self.send(kind, slot, self.up_y, source=source)

        @pl.when(self.y == 0)
        def _():
            self.send(kind, slot, self.down_y, source=source)

    def own(self, kind):
        source, slot = self.sources[kind], self.slot(kind, 0, 0)

        @pl.when(self.y < 2)
        def _():
            self.send(kind, slot, self.far_y, source=source)

        for d in (2, -2, 1, -1):
            self.send(kind, slot, self.along[d], source=source)
        self.beside(kind, slot, source)
        self.to_twin(kind, slot, source)

    def take(self, kind, dy, dz, on=(), half_on=()):
        slot = self.slot(kind, dy, dz)
        self.arrived(kind, slot, halves=dz == 4 and dy in (0, 2))
        for d in on:
            self.send(kind, slot, self.along[d])
        for d in half_on:
            self.send(kind, slot, self.along[d], half=0 if d > 0 else 1)
        if dy == 0:
            self.beside(kind, slot)
        self.to_twin(kind, slot)

    def when_far(self, *steps):
        def run():
            @pl.when(self.y >= 2)
            def _():
                for step in steps:
                    step()

        return run

    def stages(self, kind):
        take = functools.partial(self.take, kind)
        first = [functools.partial(self.own, kind)]
        near = [self.when_far(lambda: take(2, 0, (2, -2, 1, -1)))]
        near += [lambda s=s: take(0, -2 * s, (s,), (2 * s,)) for s in (1, -1)]
        near += [lambda s=s: take(0, -s) for s in (1, -1)]
        middle = [self.when_far(*(lambda s=s: take(2, -2 * s, (s,), (2 * s,)) for s in (1, -1)))]
        middle += [lambda s=s: take(0, -3 * s) for s in (1, -1)]
        middle += [lambda: take(0, 4)]
        return [first, near, middle, self.last(kind)]

    def last(self, kind):
        take = functools.partial(self.take, kind)

        def beside(*shifts):
            def run():
                @pl.when(self.y >= 1)
                def _():
                    for dz in shifts:
                        take(-1, dz)

                @pl.when(self.y == NY - 1)
                def _():
                    for dz in shifts:
                        take(1, dz)

            return run

        return [
            beside(0),
            beside(1, -1),
            self.when_far(lambda: take(2, 1), lambda: take(2, -1)),
            beside(2),
            beside(-2),
            beside(3),
            beside(-3),
            self.when_far(lambda: take(2, 3), lambda: take(2, -3)),
            beside(4),
            self.when_far(lambda: take(2, 4)),
        ]

    def by_row(self, kind, sem, blocks):
        for row, count in enumerate(blocks):

            @pl.when(self.y == row)
            def _(count=count):
                due = self.buffers[kind].at[pl.ds(0, count)]
                pltpu.make_async_copy(due, due, sem.at[kind]).wait()

    def other_half(self, kind):
        self.by_row(kind, self.twin_recv, ROW_BLOCKS)

    def sent(self):
        for kind in (0, 1):
            self.by_row(kind, self.twin_send, ROW_BLOCKS)
            self.by_row(kind, self.send_sem, SENT)


def kernel(
    vert_hbm, count_hbm, slash_hbm, q_hbm, k_hbm, v_hbm, w_hbm, out_hbm,
    keys_vm, values_vm, q_vm, w_vm, scores, weights, scale_by, att, part,
    opp_in, dir_in, sum_in, sum_out, out_vm,
    vert_ref, count_ref, slash_ref, key_at, value_at, bias_at,
    full_sem, half_sem, send_sem, twin_send, twin_recv, own_sem, q_sem, w_sem, out_sem,
    opp_sem, dir_sem, sum_sem, first_send, second_send,
):
    me, tp = lax.axis_index("seq"), lax.axis_index("tp")
    core, z, y = me % 2, (me // 2) % NZ, me // (2 * NZ)

    def seq_at(core, y, z):
        return {"seq": ((y + NY) % NY * NZ + (z + NZ) % NZ) * 2 + core}

    right, left = {"tp": (tp + 1) % 4}, {"tp": (tp + 3) % 4}
    own_key, own_value = key_slot(core, y, z), value_slot(core, y, z)
    own_copies = [
        pltpu.make_async_copy(source, target, own_sem.at[n])
        for n, (source, target) in enumerate(
            (
                (k_hbm, keys_vm.at[own_key]),
                (v_hbm, values_vm.at[own_value]),
                (vert_hbm, vert_ref),
                (count_hbm, count_ref),
                (slash_hbm, slash_ref),
            )
        )
    ]
    for copy in own_copies:
        copy.start()
    for head in range(HEADS):
        pltpu.make_async_copy(
            q_hbm.at[:, pl.ds(head * HEAD, HEAD)], q_vm.at[head], q_sem
        ).start()
    for p in range(PIECES):
        pltpu.make_async_copy(
            w_hbm.at[:, pl.ds(p * PIECE, PIECE)], w_vm.at[p], w_sem.at[p]
        ).start()

    moves = Gather(
        (keys_vm, values_vm), (full_sem, half_sem, send_sem, twin_send, twin_recv),
        (k_hbm, v_hbm), core, y, z, seq_at,
    )
    barrier = pltpu.get_barrier_semaphore()
    neighbours = (
        moves.up_y, moves.down_y, moves.far_y, moves.twin, right, left, *moves.along.values(),
    )
    for where in neighbours:
        pl.semaphore_signal(barrier, inc=1, device_id=where, device_id_type=MESH)
    pl.semaphore_wait(barrier, len(neighbours))

    keys, values = moves.stages(0), moves.stages(1)

    def do(stage):
        for handler in stage:
            handler()

    do(keys[0])
    do(values[0])
    for copy in own_copies:
        copy.wait()

    @pl.loop(0, HEADS)
    def _(head):
        choose_blocks(head, me, vert_ref, count_ref, slash_ref, key_at, value_at, bias_at)

    for stage in (keys[1], values[1], keys[2], values[2], keys[3]):
        do(stage)
    pltpu.make_async_copy(q_vm, q_vm, q_sem).wait()
    moves.other_half(0)

    def weigh(head, n):
        weigh_head(
            head, q_vm, keys_vm, key_at, bias_at, own_key, scores.at[n], weights, scale_by
        )

    ends = values[3]
    cuts = [0] + [len(ends) * c // 8 for c in CUTS] + [len(ends)]
    for n in range(HEADS // 2):
        do(ends[cuts[n] : cuts[n + 1]])
        weigh(2 * n, 0)
        weigh(2 * n + 1, 1)
    do(ends[cuts[HEADS // 2] :])
    moves.other_half(1)

    @pl.loop(0, HEADS // 2)
    def _(pair):
        for n in range(2):
            combine_head(pair * 2 + n, values_vm, value_at, own_value, weights, scale_by, att)

    def rows_of(p, target):
        return part.at[p, pl.ds(pl.multiple_of((target + 4) % 4 * ROWS, ROWS), ROWS)]

    @pl.loop(0, SIDE)
    def _(j):
        for p, ahead, behind, step in ((j, right, left, 1), (j + SIDE, left, right, -1)):
            pltpu.make_async_copy(w_vm.at[p], w_vm.at[p], w_sem.at[p]).wait()
            part[p] = jnp.dot(att[...], w_vm[p], preferred_element_type=jnp.float32).astype(
                jnp.bfloat16
            )
            remote(rows_of(p, tp + 2), opp_in.at[p], first_send, opp_sem.at[p], ahead).start()
            remote(rows_of(p, tp - step), dir_in.at[p], first_send, dir_sem.at[p], behind).start()

    @pl.loop(0, SIDE)
    def _(j):
        for p, ahead, step in ((j, right, 1), (j + SIDE, left, -1)):
            pltpu.make_async_copy(opp_in.at[p], opp_in.at[p], opp_sem.at[p]).wait()
            summed = opp_in[p].astype(jnp.float32) + rows_of(p, tp + step)[...].astype(jnp.float32)
            sum_out[p] = summed.astype(jnp.bfloat16)
            remote(sum_out.at[p], sum_in.at[p], second_send, sum_sem.at[p], ahead).start()

    for j in range(SIDE):
        for p in (j, j + SIDE):
            pltpu.make_async_copy(dir_in.at[p], dir_in.at[p], dir_sem.at[p]).wait()
            pltpu.make_async_copy(sum_in.at[p], sum_in.at[p], sum_sem.at[p]).wait()
            whole = (
                rows_of(p, tp)[...].astype(jnp.float32)
                + dir_in[p].astype(jnp.float32)
                + sum_in[p].astype(jnp.float32)
            )
            at = slice(p * PIECE, (p + 1) * PIECE)
            out_vm[:, at] = whole.astype(jnp.bfloat16)
            pltpu.make_async_copy(out_vm.at[:, at], out_hbm.at[:, at], out_sem).start()
    pltpu.make_async_copy(part.at[pl.ds(0, SIDE)], part.at[pl.ds(0, SIDE)], first_send).wait()
    pltpu.make_async_copy(sum_out, sum_out, second_send).wait()
    moves.sent()
    pltpu.make_async_copy(out_vm, out_hbm, out_sem).wait()


def body(queries, key_vectors, value_vectors, vertical, vertical_count, slash_offsets, out_weight):
    anywhere = pl.BlockSpec(memory_space=pl.ANY)
    bf16, dma = jnp.bfloat16, pltpu.SemaphoreType.DMA
    return pl.pallas_call(
        kernel,
        out_shape=jax.ShapeDtypeStruct((ROWS, D), bf16),
        in_specs=[anywhere] * 7,
        out_specs=anywhere,
        scratch_shapes=[
            pltpu.VMEM((NB, BLOCK, HEAD), bf16),
            pltpu.VMEM((NB, BLOCK, HEAD), bf16),
            pltpu.VMEM((HEADS, BLOCK, HEAD), bf16),
            pltpu.VMEM((PIECES, FEATURES, PIECE), bf16),
            pltpu.VMEM((2, BLOCK, SLOTS * BLOCK), jnp.float32),
            pltpu.VMEM((HEADS, BLOCK, SLOTS * BLOCK), bf16),
            pltpu.VMEM((HEADS, BLOCK, HEAD), jnp.float32),
            pltpu.VMEM((BLOCK, FEATURES), bf16),
            pltpu.VMEM((PIECES, BLOCK, PIECE), bf16),
            pltpu.VMEM((PIECES, ROWS, PIECE), bf16),
            pltpu.VMEM((PIECES, ROWS, PIECE), bf16),
            pltpu.VMEM((PIECES, ROWS, PIECE), bf16),
            pltpu.VMEM((PIECES, ROWS, PIECE), bf16),
            pltpu.VMEM((ROWS, D), bf16),
            pltpu.SMEM((HEADS, NVERT), jnp.int32),
            pltpu.SMEM((HEADS,), jnp.int32),
            pltpu.SMEM((HEADS, NSLASH), jnp.int32),
            pltpu.SMEM((HEADS, 32), jnp.int32),
            pltpu.SMEM((HEADS, 32), jnp.int32),
            pltpu.SMEM((HEADS, 32), jnp.float32),
            dma((2, HALF)),
            dma((2, HALF)),
            dma((2,)),
            dma((2,)),
            dma((2,)),
            dma((5,)),
            dma,
            dma((PIECES,)),
            dma,
            dma((PIECES,)),
            dma((PIECES,)),
            dma((PIECES,)),
            dma,
            dma,
        ],
        compiler_params=pltpu.CompilerParams(
            collective_id=0, has_side_effects=True, vmem_limit_bytes=64 * 1024 * 1024
        ),
        cost_estimate=pl.CostEstimate(
            flops=3_200_000_000, bytes_accessed=16_000_000, transcendentals=3_300_000
        ),
        name="attend_project",
    )(vertical, vertical_count, slash_offsets, queries, key_vectors, value_vectors, out_weight)


def solution(mesh):
    in_specs = (
        P("seq", "tp"),
        P("seq", "tp"),
        P("seq", "tp"),
        P("tp", None),
        P("tp"),
        P("tp", None),
        P("tp", None),
    )
    out_specs = P(("seq", "tp"), None)
    return jax.shard_map(body, mesh=mesh, in_specs=in_specs, out_specs=out_specs, check_vma=False)
```

```python
import functools
import math

import jax
import jax.numpy as jnp
from jax import lax
from jax.experimental import pallas as pl
from jax.experimental.pallas import tpu as pltpu
from jax.sharding import PartitionSpec as P

HEAD = 128
BLOCK = 128
HEADS = 8
NY, NZ = 4, 8
NB = 64
HALF = NB // 2
NSLASH, NVERT = 8, 16
SLOTS = 1 + NSLASH + NVERT
D = 5120
PIECE = 512
SIDE = D // PIECE // 2
PIECES = 2 * SIDE
ROWS = 32
FEATURES = HEADS * HEAD
EXP2_SCALE = HEAD**-0.5 * math.log2(math.e)
MESH = pl.DeviceIdType.MESH
CUTS = (2, 4, 6, 8)
ROW_BLOCKS = tuple(NZ * (row + 1) for row in range(NY))
SENT = (24, 16, 22, 14)
HOPS_Z = (0, 1, 1, 2, 2)
NEG = float("-inf")


def key_slot(core, y, z):
    return core * HALF + z * NY + y


def value_slot(core, y, z):
    return core * HALF + y * NZ + z


def choose_blocks(head, me, vert_ref, count_ref, slash_ref, key_at, value_at, bias_at):
    low = jnp.where(me < 32, jnp.left_shift(jnp.int32(1), me % 32), 0)
    high = jnp.where(me < 32, 0, jnp.left_shift(jnp.int32(1), me % 32))
    count = count_ref[head]
    for c in range(1, SLOTS):
        if c <= NSLASH:
            block = me - slash_ref[head, c - 1]
            usable = block >= 0
        else:
            block = vert_ref[head, c - 1 - NSLASH]
            usable = (block <= me) & (c - 1 - NSLASH < count)
        block = jnp.where(usable, block, me)
        bit = jnp.left_shift(jnp.int32(1), block % 32)
        in_low = block < 32
        seen = (jnp.where(in_low, low, high) & bit) != 0
        kept = usable & jnp.logical_not(seen)
        add = jnp.where(kept, bit, 0)
        low = low | jnp.where(in_low, add, 0)
        high = high | jnp.where(in_low, 0, add)
        core, z, y = block % 2, (block // 2) % NZ, block // (2 * NZ)
        key_at[head, c] = key_slot(core, y, z)
        value_at[head, c] = value_slot(core, y, z)
        bias_at[head, c] = jnp.where(kept, jnp.float32(0), jnp.float32(NEG))


def slot_groups(size):
    return [list(range(c, min(c + size, SLOTS))) for c in range(0, SLOTS, size)]


def weigh_head(head, q_vm, keys_vm, key_at, bias_at, own_key, scores, weights, scale_by):
    query = q_vm[head]
    rows = lax.broadcasted_iota(jnp.int32, (BLOCK, BLOCK), 0)
    cols = lax.broadcasted_iota(jnp.int32, (BLOCK, BLOCK), 1)
    top = None
    for slots in slot_groups(2):
        keys = [keys_vm[own_key if s == 0 else key_at[head, s]] for s in slots]
        keys = keys[0] if len(keys) == 1 else jnp.concatenate(keys, axis=0)
        both = lax.dot_general(
            query, keys, (((1,), (1,)), ((), ())), preferred_element_type=jnp.float32
        )
        for n, s in enumerate(slots):
            part = both[:, n * BLOCK : (n + 1) * BLOCK]
            if s == 0:
                part = jnp.where(cols <= rows, part, NEG)
            else:
                part = part + bias_at[head, s]
            scores[:, s * BLOCK : (s + 1) * BLOCK] = part
            top = part if top is None else jnp.maximum(top, part)
    top = jnp.max(top, axis=1, keepdims=True)
    total = None
    for s in range(SLOTS):
        at = slice(s * BLOCK, (s + 1) * BLOCK)
        part = jnp.exp2((scores[:, at] - top) * EXP2_SCALE)
        weights[head, :, at] = part.astype(jnp.bfloat16)
        total = part if total is None else total + part
    total = jnp.sum(total, axis=1, keepdims=True)
    scale_by[head] = jnp.broadcast_to(1.0 / total, (BLOCK, HEAD))


def combine_head(head, values_vm, value_at, own_value, weights, scale_by, att):
    out = None
    for slots in slot_groups(4):
        values = [values_vm[own_value if s == 0 else value_at[head, s]] for s in slots]
        values = values[0] if len(values) == 1 else jnp.concatenate(values, axis=0)
        part = weights[head, :, slots[0] * BLOCK : (slots[-1] + 1) * BLOCK]
        term = jnp.dot(part, values, preferred_element_type=jnp.float32)
        out = term if out is None else out + term
    out = out * scale_by[head]
    att[:, pl.ds(pl.multiple_of(head * HEAD, HEAD), HEAD)] = out.astype(jnp.bfloat16)


def remote(src, dst, send, recv, where):
    return pltpu.make_async_remote_copy(
        src_ref=src, dst_ref=dst, send_sem=send, recv_sem=recv, device_id=where, device_id_type=MESH
    )


class Gather:
    def __init__(self, buffers, sems, sources, core, y, z, seq_at):
        self.buffers, self.sources, self.core, self.y, self.z = buffers, sources, core, y, z
        self.full_sem, self.half_sem, self.send_sem, self.twin_send, self.twin_recv = sems
        other = 1 - core
        self.up_y, self.down_y = seq_at(other, y + 1, z), seq_at(other, y - 1, z)
        self.far_y = seq_at(other, y + 2, z)
        self.along = {d: seq_at(other, y, z + d) for d in (-2, -1, 1, 2)}
        self.twin = seq_at(1 - core, y, z)

    def slot(self, kind, dy, dz):
        hops = HOPS_Z[abs(dz)] + (dy in (1, -1)) if abs(dy) < 2 else 1 + HOPS_Z[abs(dz)]
        core = self.core if hops % 2 == 0 else 1 - self.core
        at = key_slot if kind == 0 else value_slot
        return at(core, (self.y + dy + NY) % NY, (self.z + dz + NZ) % NZ)

    def send(self, kind, slot, where, half=None, source=None):
        target = self.buffers[kind].at[slot]
        source = target if source is None else source
        if half is not None:
            source = source.at[pl.ds(half * 64, 64)]
            target = target.at[pl.ds(half * 64, 64)]
        recv = (self.half_sem if half == 1 else self.full_sem).at[kind, slot % HALF]
        remote(source, target, self.send_sem.at[kind], recv, where).start()

    def to_twin(self, kind, slot, source=None):
        target = self.buffers[kind].at[slot]
        source = target if source is None else source
        send, recv = self.twin_send.at[kind], self.twin_recv.at[kind]
        remote(source, target, send, recv, self.twin).start()

    def arrived(self, kind, slot, halves=False):
        whole = self.buffers[kind].at[slot]
        if halves:
            for half, sem in ((0, self.full_sem), (1, self.half_sem)):
                piece = whole.at[pl.ds(half * 64, 64)]
                pltpu.make_async_copy(piece, piece, sem.at[kind, slot % HALF]).wait()
        else:
            pltpu.make_async_copy(whole, whole, self.full_sem.at[kind, slot % HALF]).wait()

    def beside(self, kind, slot, source=None):
        @pl.when(self.y < NY - 1)
        def _():
            self.send(kind, slot, self.up_y, source=source)

        @pl.when(self.y == 0)
        def _():
            self.send(kind, slot, self.down_y, source=source)

    def own(self, kind):
        source, slot = self.sources[kind], self.slot(kind, 0, 0)

        @pl.when(self.y < 2)
        def _():
            self.send(kind, slot, self.far_y, source=source)

        for d in (2, -2, 1, -1):
            self.send(kind, slot, self.along[d], source=source)
        self.beside(kind, slot, source)
        self.to_twin(kind, slot, source)

    def take(self, kind, dy, dz, on=(), half_on=()):
        slot = self.slot(kind, dy, dz)
        self.arrived(kind, slot, halves=dz == 4 and dy in (0, 2))
        for d in on:
            self.send(kind, slot, self.along[d])
        for d in half_on:
            self.send(kind, slot, self.along[d], half=0 if d > 0 else 1)
        if dy == 0:
            self.beside(kind, slot)
        self.to_twin(kind, slot)

    def when_far(self, *steps):
        def run():
            @pl.when(self.y >= 2)
            def _():
                for step in steps:
                    step()

        return run

    def stages(self, kind):
        take = functools.partial(self.take, kind)
        first = [functools.partial(self.own, kind)]
        near = [self.when_far(lambda: take(2, 0, (2, -2, 1, -1)))]
        near += [lambda s=s: take(0, -2 * s, (s,), (2 * s,)) for s in (1, -1)]
        near += [lambda s=s: take(0, -s) for s in (1, -1)]
        middle = [self.when_far(*(lambda s=s: take(2, -2 * s, (s,), (2 * s,)) for s in (1, -1)))]
        middle += [lambda s=s: take(0, -3 * s) for s in (1, -1)]
        middle += [lambda: take(0, 4)]
        return [first, near, middle, self.last(kind)]

    def last(self, kind):
        take = functools.partial(self.take, kind)

        def beside(*shifts):
            def run():
                @pl.when(self.y >= 1)
                def _():
                    for dz in shifts:
                        take(-1, dz)

                @pl.when(self.y == NY - 1)
                def _():
                    for dz in shifts:
                        take(1, dz)

            return run

        return [
            beside(0),
            beside(1, -1),
            self.when_far(lambda: take(2, 1), lambda: take(2, -1)),
            beside(2),
            beside(-2),
            beside(3),
            beside(-3),
            self.when_far(lambda: take(2, 3), lambda: take(2, -3)),
            beside(4),
            self.when_far(lambda: take(2, 4)),
        ]

    def by_row(self, kind, sem, blocks):
        for row, count in enumerate(blocks):

            @pl.when(self.y == row)
            def _(count=count):
                due = self.buffers[kind].at[pl.ds(0, count)]
                pltpu.make_async_copy(due, due, sem.at[kind]).wait()

    def other_half(self, kind):
        self.by_row(kind, self.twin_recv, ROW_BLOCKS)

    def sent(self):
        for kind in (0, 1):
            self.by_row(kind, self.twin_send, ROW_BLOCKS)
            self.by_row(kind, self.send_sem, SENT)


def kernel(
    vert_hbm, count_hbm, slash_hbm, q_hbm, k_hbm, v_hbm, w_hbm, out_ref,
    keys_vm, values_vm, q_vm, w_vm, scores, weights, scale_by, att, part,
    opp_in, dir_in, sum_in, sum_out,
    vert_ref, count_ref, slash_ref, key_at, value_at, bias_at,
    full_sem, half_sem, send_sem, twin_send, twin_recv, own_sem, q_sem, w_sem,
    opp_sem, dir_sem, sum_sem, first_send, second_send,
):
    me, tp = lax.axis_index("seq"), lax.axis_index("tp")
    core, z, y = me % 2, (me // 2) % NZ, me // (2 * NZ)

    def seq_at(core, y, z):
        return {"seq": ((y + NY) % NY * NZ + (z + NZ) % NZ) * 2 + core}

    right, left = {"tp": (tp + 1) % 4}, {"tp": (tp + 3) % 4}
    own_key, own_value = key_slot(core, y, z), value_slot(core, y, z)
    own_copies = [
        pltpu.make_async_copy(source, target, own_sem.at[n])
        for n, (source, target) in enumerate(
            (
                (k_hbm, keys_vm.at[own_key]),
                (v_hbm, values_vm.at[own_value]),
                (vert_hbm, vert_ref),
                (count_hbm, count_ref),
                (slash_hbm, slash_ref),
            )
        )
    ]
    for copy in own_copies:
        copy.start()
    for head in range(HEADS):
        pltpu.make_async_copy(
            q_hbm.at[:, pl.ds(head * HEAD, HEAD)], q_vm.at[head], q_sem
        ).start()
    for p in range(PIECES):
        pltpu.make_async_copy(
            w_hbm.at[:, pl.ds(p * PIECE, PIECE)], w_vm.at[p], w_sem.at[p]
        ).start()

    moves = Gather(
        (keys_vm, values_vm), (full_sem, half_sem, send_sem, twin_send, twin_recv),
        (k_hbm, v_hbm), core, y, z, seq_at,
    )
    barrier = pltpu.get_barrier_semaphore()
    neighbours = (
        moves.up_y, moves.down_y, moves.far_y, moves.twin, right, left, *moves.along.values(),
    )
    for where in neighbours:
        pl.semaphore_signal(barrier, inc=1, device_id=where, device_id_type=MESH)
    pl.semaphore_wait(barrier, len(neighbours))

    keys, values = moves.stages(0), moves.stages(1)

    def do(stage):
        for handler in stage:
            handler()

    do(keys[0])
    do(values[0])
    for copy in own_copies:
        copy.wait()

    @pl.loop(0, HEADS)
    def _(head):
        choose_blocks(head, me, vert_ref, count_ref, slash_ref, key_at, value_at, bias_at)

    for stage in (keys[1], values[1], keys[2], values[2], keys[3]):
        do(stage)
    pltpu.make_async_copy(q_vm, q_vm, q_sem).wait()
    moves.other_half(0)

    def weigh(head, n):
        weigh_head(
            head, q_vm, keys_vm, key_at, bias_at, own_key, scores.at[n], weights, scale_by
        )

    ends = values[3]
    cuts = [0] + [len(ends) * c // 8 for c in CUTS] + [len(ends)]
    for n in range(HEADS // 2):
        do(ends[cuts[n] : cuts[n + 1]])
        weigh(2 * n, 0)
        weigh(2 * n + 1, 1)
    do(ends[cuts[HEADS // 2] :])
    moves.other_half(1)

    @pl.loop(0, HEADS // 2)
    def _(pair):
        for n in range(2):
            combine_head(pair * 2 + n, values_vm, value_at, own_value, weights, scale_by, att)

    def rows_of(p, target):
        return part.at[p, pl.ds(pl.multiple_of((target + 4) % 4 * ROWS, ROWS), ROWS)]

    @pl.loop(0, SIDE)
    def _(j):
        for p, ahead, behind, step in ((j, right, left, 1), (j + SIDE, left, right, -1)):
            pltpu.make_async_copy(w_vm.at[p], w_vm.at[p], w_sem.at[p]).wait()
            part[p] = jnp.dot(att[...], w_vm[p], preferred_element_type=jnp.float32).astype(
                jnp.bfloat16
            )
            remote(rows_of(p, tp + 2), opp_in.at[p], first_send, opp_sem.at[p], ahead).start()
            remote(rows_of(p, tp - step), dir_in.at[p], first_send, dir_sem.at[p], behind).start()

    @pl.loop(0, SIDE)
    def _(j):
        for p, ahead, step in ((j, right, 1), (j + SIDE, left, -1)):
            pltpu.make_async_copy(opp_in.at[p], opp_in.at[p], opp_sem.at[p]).wait()
            summed = opp_in[p].astype(jnp.float32) + rows_of(p, tp + step)[...].astype(jnp.float32)
            sum_out[p] = summed.astype(jnp.bfloat16)
            remote(sum_out.at[p], sum_in.at[p], second_send, sum_sem.at[p], ahead).start()

    for j in range(SIDE):
        for p in (j, j + SIDE):
            pltpu.make_async_copy(dir_in.at[p], dir_in.at[p], dir_sem.at[p]).wait()
            pltpu.make_async_copy(sum_in.at[p], sum_in.at[p], sum_sem.at[p]).wait()
            whole = (
                rows_of(p, tp)[...].astype(jnp.float32)
                + dir_in[p].astype(jnp.float32)
                + sum_in[p].astype(jnp.float32)
            )
            out_ref[:, p * PIECE : (p + 1) * PIECE] = whole.astype(jnp.bfloat16)
    pltpu.make_async_copy(part.at[pl.ds(0, SIDE)], part.at[pl.ds(0, SIDE)], first_send).wait()
    pltpu.make_async_copy(sum_out, sum_out, second_send).wait()
    moves.sent()


def body(queries, key_vectors, value_vectors, vertical, vertical_count, slash_offsets, out_weight):
    anywhere = pl.BlockSpec(memory_space=pl.ANY)
    bf16, dma = jnp.bfloat16, pltpu.SemaphoreType.DMA
    inputs = (
        vertical, vertical_count, slash_offsets, queries, key_vectors, value_vectors, out_weight
    )
    return pl.pallas_call(
        kernel,
        out_shape=jax.ShapeDtypeStruct((ROWS, D), bf16),
        in_specs=[anywhere] * 7,
        out_specs=pl.BlockSpec(memory_space=pltpu.VMEM),
        scratch_shapes=[
            pltpu.VMEM((NB, BLOCK, HEAD), bf16),
            pltpu.VMEM((NB, BLOCK, HEAD), bf16),
            pltpu.VMEM((HEADS, BLOCK, HEAD), bf16),
            pltpu.VMEM((PIECES, FEATURES, PIECE), bf16),
            pltpu.VMEM((2, BLOCK, SLOTS * BLOCK), jnp.float32),
            pltpu.VMEM((HEADS, BLOCK, SLOTS * BLOCK), bf16),
            pltpu.VMEM((HEADS, BLOCK, HEAD), jnp.float32),
            pltpu.VMEM((BLOCK, FEATURES), bf16),
            pltpu.VMEM((PIECES, BLOCK, PIECE), bf16),
            pltpu.VMEM((PIECES, ROWS, PIECE), bf16),
            pltpu.VMEM((PIECES, ROWS, PIECE), bf16),
            pltpu.VMEM((PIECES, ROWS, PIECE), bf16),
            pltpu.VMEM((PIECES, ROWS, PIECE), bf16),
            pltpu.SMEM((HEADS, NVERT), jnp.int32),
            pltpu.SMEM((HEADS,), jnp.int32),
            pltpu.SMEM((HEADS, NSLASH), jnp.int32),
            pltpu.SMEM((HEADS, 32), jnp.int32),
            pltpu.SMEM((HEADS, 32), jnp.int32),
            pltpu.SMEM((HEADS, 32), jnp.float32),
            dma((2, HALF)),
            dma((2, HALF)),
            dma((2,)),
            dma((2,)),
            dma((2,)),
            dma((5,)),
            dma,
            dma((PIECES,)),
            dma((PIECES,)),
            dma((PIECES,)),
            dma((PIECES,)),
            dma,
            dma,
        ],
        compiler_params=pltpu.CompilerParams(
            collective_id=0, has_side_effects=True, vmem_limit_bytes=48 * 1024 * 1024
        ),
        cost_estimate=pl.CostEstimate(
            flops=3_200_000_000, bytes_accessed=16_000_000, transcendentals=3_300_000
        ),
        name="attend_project",
    )(*[pltpu.with_memory_space_constraint(a, pltpu.HBM) for a in inputs])


def solution(mesh):
    in_specs = (
        P("seq", "tp"),
        P("seq", "tp"),
        P("seq", "tp"),
        P("tp", None),
        P("tp"),
        P("tp", None),
        P("tp", None),
    )
    out_specs = P(("seq", "tp"), None)
    return jax.shard_map(body, mesh=mesh, in_specs=in_specs, out_specs=out_specs, check_vma=False)
```

```python
import functools
import math

import jax
import jax.numpy as jnp
from jax import lax
from jax.experimental import pallas as pl
from jax.experimental.pallas import tpu as pltpu
from jax.sharding import PartitionSpec as P

HEAD = 128
BLOCK = 128
HEADS = 8
NY, NZ = 4, 8
NB = 64
HALF = NB // 2
NSLASH, NVERT = 8, 16
SLOTS = 1 + NSLASH + NVERT
D = 5120
PIECE = 512
SIDE = D // PIECE // 2
PIECES = 2 * SIDE
ROWS = 32
FEATURES = HEADS * HEAD
EXP2_SCALE = HEAD**-0.5 * math.log2(math.e)
MESH = pl.DeviceIdType.MESH
CUTS = (2, 4, 6, 8)
ROW_BLOCKS = tuple(NZ * (row + 1) for row in range(NY))
SENT = (24, 16, 22, 14)
HOPS_Z = (0, 1, 1, 2, 2)
NEG = float("-inf")


def key_slot(core, y, z):
    return core * HALF + z * NY + y


def value_slot(core, y, z):
    return core * HALF + y * NZ + z


def choose_blocks(head, me, vert_ref, count_ref, slash_ref, key_at, value_at, bias_at):
    low = jnp.where(me < 32, jnp.left_shift(jnp.int32(1), me % 32), 0)
    high = jnp.where(me < 32, 0, jnp.left_shift(jnp.int32(1), me % 32))
    count = count_ref[head]
    for c in range(1, SLOTS):
        if c <= NSLASH:
            block = me - slash_ref[head, c - 1]
            usable = block >= 0
        else:
            block = vert_ref[head, c - 1 - NSLASH]
            usable = (block <= me) & (c - 1 - NSLASH < count)
        block = jnp.where(usable, block, me)
        bit = jnp.left_shift(jnp.int32(1), block % 32)
        in_low = block < 32
        seen = (jnp.where(in_low, low, high) & bit) != 0
        kept = usable & jnp.logical_not(seen)
        add = jnp.where(kept, bit, 0)
        low = low | jnp.where(in_low, add, 0)
        high = high | jnp.where(in_low, 0, add)
        core, z, y = block % 2, (block // 2) % NZ, block // (2 * NZ)
        key_at[head, c] = key_slot(core, y, z)
        value_at[head, c] = value_slot(core, y, z)
        bias_at[head, c] = jnp.where(kept, jnp.float32(0), jnp.float32(NEG))


def slot_groups(size):
    return [list(range(c, min(c + size, SLOTS))) for c in range(0, SLOTS, size)]


def weigh_head(head, q_vm, keys_vm, key_at, bias_at, own_key, scores, weights, scale_by):
    query = q_vm[head]
    rows = lax.broadcasted_iota(jnp.int32, (BLOCK, BLOCK), 0)
    cols = lax.broadcasted_iota(jnp.int32, (BLOCK, BLOCK), 1)
    top = None
    for slots in slot_groups(2):
        keys = [keys_vm[own_key if s == 0 else key_at[head, s]] for s in slots]
        keys = keys[0] if len(keys) == 1 else jnp.concatenate(keys, axis=0)
        both = lax.dot_general(
            query, keys, (((1,), (1,)), ((), ())), preferred_element_type=jnp.float32
        )
        for n, s in enumerate(slots):
            part = both[:, n * BLOCK : (n + 1) * BLOCK]
            if s == 0:
                part = jnp.where(cols <= rows, part, NEG)
            else:
                part = part + bias_at[head, s]
            scores[:, s * BLOCK : (s + 1) * BLOCK] = part
            top = part if top is None else jnp.maximum(top, part)
    top = jnp.max(top, axis=1, keepdims=True)
    total = None
    for s in range(SLOTS):
        at = slice(s * BLOCK, (s + 1) * BLOCK)
        part = jnp.exp2((scores[:, at] - top) * EXP2_SCALE)
        weights[head, :, at] = part.astype(jnp.bfloat16)
        total = part if total is None else total + part
    total = jnp.sum(total, axis=1, keepdims=True)
    scale_by[head] = jnp.broadcast_to(1.0 / total, (BLOCK, HEAD))


def combine_head(head, half, starts, values_vm, value_at, own_value, weights, scale_by, att):
    def of_targets(ref, at):
        return jnp.concatenate([ref[head, pl.ds(start, ROWS), at] for start in starts], axis=0)

    out = None
    for slots in slot_groups(4):
        values = [values_vm[own_value if s == 0 else value_at[head, s]] for s in slots]
        values = values[0] if len(values) == 1 else jnp.concatenate(values, axis=0)
        part = of_targets(weights, slice(slots[0] * BLOCK, (slots[-1] + 1) * BLOCK))
        term = jnp.dot(part, values, preferred_element_type=jnp.float32)
        out = term if out is None else out + term
    out = out * of_targets(scale_by, slice(0, HEAD))
    att[half, :, pl.ds(pl.multiple_of(head * HEAD, HEAD), HEAD)] = out.astype(jnp.bfloat16)


def remote(src, dst, send, recv, where):
    return pltpu.make_async_remote_copy(
        src_ref=src, dst_ref=dst, send_sem=send, recv_sem=recv, device_id=where, device_id_type=MESH
    )


class Gather:
    def __init__(self, buffers, sems, sources, core, y, z, seq_at):
        self.buffers, self.sources, self.core, self.y, self.z = buffers, sources, core, y, z
        self.full_sem, self.half_sem, self.send_sem, self.twin_send, self.twin_recv = sems
        other = 1 - core
        self.up_y, self.down_y = seq_at(other, y + 1, z), seq_at(other, y - 1, z)
        self.far_y = seq_at(other, y + 2, z)
        self.along = {d: seq_at(other, y, z + d) for d in (-2, -1, 1, 2)}
        self.twin = seq_at(1 - core, y, z)

    def slot(self, kind, dy, dz):
        hops = HOPS_Z[abs(dz)] + (dy in (1, -1)) if abs(dy) < 2 else 1 + HOPS_Z[abs(dz)]
        core = self.core if hops % 2 == 0 else 1 - self.core
        at = key_slot if kind == 0 else value_slot
        return at(core, (self.y + dy + NY) % NY, (self.z + dz + NZ) % NZ)

    def send(self, kind, slot, where, half=None, source=None):
        target = self.buffers[kind].at[slot]
        source = target if source is None else source
        if half is not None:
            source = source.at[pl.ds(half * 64, 64)]
            target = target.at[pl.ds(half * 64, 64)]
        recv = (self.half_sem if half == 1 else self.full_sem).at[kind, slot % HALF]
        remote(source, target, self.send_sem.at[kind], recv, where).start()

    def to_twin(self, kind, slot, source=None):
        target = self.buffers[kind].at[slot]
        source = target if source is None else source
        send, recv = self.twin_send.at[kind], self.twin_recv.at[kind]
        remote(source, target, send, recv, self.twin).start()

    def arrived(self, kind, slot, halves=False):
        whole = self.buffers[kind].at[slot]
        if halves:
            for half, sem in ((0, self.full_sem), (1, self.half_sem)):
                piece = whole.at[pl.ds(half * 64, 64)]
                pltpu.make_async_copy(piece, piece, sem.at[kind, slot % HALF]).wait()
        else:
            pltpu.make_async_copy(whole, whole, self.full_sem.at[kind, slot % HALF]).wait()

    def beside(self, kind, slot, source=None):
        @pl.when(self.y < NY - 1)
        def _():
            self.send(kind, slot, self.up_y, source=source)

        @pl.when(self.y == 0)
        def _():
            self.send(kind, slot, self.down_y, source=source)

    def own(self, kind):
        source, slot = self.sources[kind], self.slot(kind, 0, 0)

        @pl.when(self.y < 2)
        def _():
            self.send(kind, slot, self.far_y, source=source)

        for d in (2, -2, 1, -1):
            self.send(kind, slot, self.along[d], source=source)
        self.beside(kind, slot, source)
        self.to_twin(kind, slot, source)

    def take(self, kind, dy, dz, on=(), half_on=()):
        slot = self.slot(kind, dy, dz)
        self.arrived(kind, slot, halves=dz == 4 and dy in (0, 2))
        for d in on:
            self.send(kind, slot, self.along[d])
        for d in half_on:
            self.send(kind, slot, self.along[d], half=0 if d > 0 else 1)
        if dy == 0:
            self.beside(kind, slot)
        self.to_twin(kind, slot)

    def when_far(self, *steps):
        def run():
            @pl.when(self.y >= 2)
            def _():
                for step in steps:
                    step()

        return run

    def stages(self, kind):
        take = functools.partial(self.take, kind)
        first = [functools.partial(self.own, kind)]
        near = [self.when_far(lambda: take(2, 0, (2, -2, 1, -1)))]
        near += [lambda s=s: take(0, -2 * s, (s,), (2 * s,)) for s in (1, -1)]
        near += [lambda s=s: take(0, -s) for s in (1, -1)]
        middle = [self.when_far(*(lambda s=s: take(2, -2 * s, (s,), (2 * s,)) for s in (1, -1)))]
        middle += [lambda s=s: take(0, -3 * s) for s in (1, -1)]
        middle += [lambda: take(0, 4)]
        return [first, near, middle, self.last(kind)]

    def last(self, kind):
        take = functools.partial(self.take, kind)

        def beside(*shifts):
            def run():
                @pl.when(self.y >= 1)
                def _():
                    for dz in shifts:
                        take(-1, dz)

                @pl.when(self.y == NY - 1)
                def _():
                    for dz in shifts:
                        take(1, dz)

            return run

        return [
            beside(0),
            beside(1, -1),
            self.when_far(lambda: take(2, 1), lambda: take(2, -1)),
            beside(2),
            beside(-2),
            beside(3),
            beside(-3),
            self.when_far(lambda: take(2, 3), lambda: take(2, -3)),
            beside(4),
            self.when_far(lambda: take(2, 4)),
        ]

    def by_row(self, kind, sem, blocks):
        for row, count in enumerate(blocks):

            @pl.when(self.y == row)
            def _(count=count):
                due = self.buffers[kind].at[pl.ds(0, count)]
                pltpu.make_async_copy(due, due, sem.at[kind]).wait()

    def other_half(self, kind):
        self.by_row(kind, self.twin_recv, ROW_BLOCKS)

    def sent(self):
        for kind in (0, 1):
            self.by_row(kind, self.twin_send, ROW_BLOCKS)
            self.by_row(kind, self.send_sem, SENT)


def kernel(
    vert_hbm, count_hbm, slash_hbm, q_hbm, k_hbm, v_hbm, w_hbm, out_ref,
    keys_vm, values_vm, q_vm, w_vm, scores, weights, scale_by, att, part,
    opp_in, dir_in, sum_in, sum_out,
    vert_ref, count_ref, slash_ref, key_at, value_at, bias_at,
    full_sem, half_sem, send_sem, twin_send, twin_recv, own_sem, q_sem, w_sem,
    opp_sem, dir_sem, sum_sem, first_send, second_send,
):
    me, tp = lax.axis_index("seq"), lax.axis_index("tp")
    core, z, y = me % 2, (me // 2) % NZ, me // (2 * NZ)

    def seq_at(core, y, z):
        return {"seq": ((y + NY) % NY * NZ + (z + NZ) % NZ) * 2 + core}

    right, left = {"tp": (tp + 1) % 4}, {"tp": (tp + 3) % 4}
    own_key, own_value = key_slot(core, y, z), value_slot(core, y, z)
    own_copies = [
        pltpu.make_async_copy(source, target, own_sem.at[n])
        for n, (source, target) in enumerate(
            (
                (k_hbm, keys_vm.at[own_key]),
                (v_hbm, values_vm.at[own_value]),
                (vert_hbm, vert_ref),
                (count_hbm, count_ref),
                (slash_hbm, slash_ref),
            )
        )
    ]
    for copy in own_copies:
        copy.start()
    for head in range(HEADS):
        pltpu.make_async_copy(
            q_hbm.at[:, pl.ds(head * HEAD, HEAD)], q_vm.at[head], q_sem
        ).start()
    for p in range(PIECES):
        pltpu.make_async_copy(
            w_hbm.at[:, pl.ds(p * PIECE, PIECE)], w_vm.at[p], w_sem.at[p]
        ).start()

    moves = Gather(
        (keys_vm, values_vm), (full_sem, half_sem, send_sem, twin_send, twin_recv),
        (k_hbm, v_hbm), core, y, z, seq_at,
    )
    barrier = pltpu.get_barrier_semaphore()
    neighbours = (
        moves.up_y, moves.down_y, moves.far_y, moves.twin, right, left, *moves.along.values(),
    )
    for where in neighbours:
        pl.semaphore_signal(barrier, inc=1, device_id=where, device_id_type=MESH)
    pl.semaphore_wait(barrier, len(neighbours))

    keys, values = moves.stages(0), moves.stages(1)

    def do(stage):
        for handler in stage:
            handler()

    do(keys[0])
    do(values[0])
    for copy in own_copies:
        copy.wait()

    @pl.loop(0, HEADS)
    def _(head):
        choose_blocks(head, me, vert_ref, count_ref, slash_ref, key_at, value_at, bias_at)

    for stage in (keys[1], values[1], keys[2], values[2], keys[3]):
        do(stage)
    pltpu.make_async_copy(q_vm, q_vm, q_sem).wait()
    moves.other_half(0)

    def weigh(head, n):
        weigh_head(
            head, q_vm, keys_vm, key_at, bias_at, own_key, scores.at[n], weights, scale_by
        )

    ends = values[3]
    cuts = [0] + [len(ends) * c // 8 for c in CUTS] + [len(ends)]
    for n in range(HEADS // 2):
        do(ends[cuts[n] : cuts[n + 1]])
        weigh(2 * n, 0)
        weigh(2 * n + 1, 1)
    do(ends[cuts[HEADS // 2] :])
    moves.other_half(1)

    starts = [
        [pl.multiple_of((tp + ahead) % 4 * ROWS, ROWS) for ahead in pair]
        for pair in ((2, 1), (3, 0))
    ]
    first, second = pl.ds(0, ROWS), pl.ds(ROWS, ROWS)

    def project(half, p):
        part[half, p] = jnp.dot(
            att[half], w_vm[p], preferred_element_type=jnp.float32
        ).astype(jnp.bfloat16)

    def combine(half):
        @pl.loop(0, HEADS // 2)
        def _(pair):
            for n in range(2):
                combine_head(
                    pair * 2 + n, half, starts[half], values_vm, value_at, own_value,
                    weights, scale_by, att,
                )

    def send_direct(half, rows, p, where):
        remote(part.at[half, p, rows], dir_in.at[p], first_send, dir_sem.at[p], where).start()

    combine(0)

    @pl.loop(0, SIDE)
    def _(j):
        for p, ahead in ((j, right), (j + SIDE, left)):
            pltpu.make_async_copy(w_vm.at[p], w_vm.at[p], w_sem.at[p]).wait()
            project(0, p)
            remote(part.at[0, p, first], opp_in.at[p], first_send, opp_sem.at[p], ahead).start()
        send_direct(0, second, j + SIDE, right)

    combine(1)

    @pl.loop(0, SIDE)
    def _(j):
        project(1, j)
        send_direct(1, first, j, left)
        project(1, j + SIDE)

    @pl.loop(0, SIDE)
    def _(j):
        for p, ahead, half, rows in ((j, right, 0, second), (j + SIDE, left, 1, first)):
            pltpu.make_async_copy(opp_in.at[p], opp_in.at[p], opp_sem.at[p]).wait()
            summed = opp_in[p].astype(jnp.float32) + part[half, p, rows].astype(jnp.float32)
            sum_out[p] = summed.astype(jnp.bfloat16)
            remote(sum_out.at[p], sum_in.at[p], second_send, sum_sem.at[p], ahead).start()

    for j in range(SIDE):
        for p in (j, j + SIDE):
            pltpu.make_async_copy(dir_in.at[p], dir_in.at[p], dir_sem.at[p]).wait()
            pltpu.make_async_copy(sum_in.at[p], sum_in.at[p], sum_sem.at[p]).wait()
            whole = (
                part[1, p, second].astype(jnp.float32)
                + dir_in[p].astype(jnp.float32)
                + sum_in[p].astype(jnp.float32)
            )
            out_ref[:, p * PIECE : (p + 1) * PIECE] = whole.astype(jnp.bfloat16)
    pltpu.make_async_copy(part.at[0], part.at[0], first_send).wait()
    pltpu.make_async_copy(sum_out, sum_out, second_send).wait()
    moves.sent()


def body(queries, key_vectors, value_vectors, vertical, vertical_count, slash_offsets, out_weight):
    anywhere = pl.BlockSpec(memory_space=pl.ANY)
    bf16, dma = jnp.bfloat16, pltpu.SemaphoreType.DMA
    inputs = (
        vertical, vertical_count, slash_offsets, queries, key_vectors, value_vectors, out_weight
    )
    return pl.pallas_call(
        kernel,
        out_shape=jax.ShapeDtypeStruct((ROWS, D), bf16),
        in_specs=[anywhere] * 7,
        out_specs=pl.BlockSpec(memory_space=pltpu.VMEM),
        scratch_shapes=[
            pltpu.VMEM((NB, BLOCK, HEAD), bf16),
            pltpu.VMEM((NB, BLOCK, HEAD), bf16),
            pltpu.VMEM((HEADS, BLOCK, HEAD), bf16),
            pltpu.VMEM((PIECES, FEATURES, PIECE), bf16),
            pltpu.VMEM((2, BLOCK, SLOTS * BLOCK), jnp.float32),
            pltpu.VMEM((HEADS, BLOCK, SLOTS * BLOCK), bf16),
            pltpu.VMEM((HEADS, BLOCK, HEAD), jnp.float32),
            pltpu.VMEM((2, 2 * ROWS, FEATURES), bf16),
            pltpu.VMEM((2, PIECES, 2 * ROWS, PIECE), bf16),
            pltpu.VMEM((PIECES, ROWS, PIECE), bf16),
            pltpu.VMEM((PIECES, ROWS, PIECE), bf16),
            pltpu.VMEM((PIECES, ROWS, PIECE), bf16),
            pltpu.VMEM((PIECES, ROWS, PIECE), bf16),
            pltpu.SMEM((HEADS, NVERT), jnp.int32),
            pltpu.SMEM((HEADS,), jnp.int32),
            pltpu.SMEM((HEADS, NSLASH), jnp.int32),
            pltpu.SMEM((HEADS, 32), jnp.int32),
            pltpu.SMEM((HEADS, 32), jnp.int32),
            pltpu.SMEM((HEADS, 32), jnp.float32),
            dma((2, HALF)),
            dma((2, HALF)),
            dma((2,)),
            dma((2,)),
            dma((2,)),
            dma((5,)),
            dma,
            dma((PIECES,)),
            dma((PIECES,)),
            dma((PIECES,)),
            dma((PIECES,)),
            dma,
            dma,
        ],
        compiler_params=pltpu.CompilerParams(
            collective_id=0, has_side_effects=True, vmem_limit_bytes=48 * 1024 * 1024
        ),
        cost_estimate=pl.CostEstimate(
            flops=3_200_000_000, bytes_accessed=16_000_000, transcendentals=3_300_000
        ),
        name="attend_project",
    )(*[pltpu.with_memory_space_constraint(a, pltpu.HBM) for a in inputs])


def solution(mesh):
    in_specs = (
        P("seq", "tp"),
        P("seq", "tp"),
        P("seq", "tp"),
        P("tp", None),
        P("tp"),
        P("tp", None),
        P("tp", None),
    )
    out_specs = P(("seq", "tp"), None)
    return jax.shard_map(body, mesh=mesh, in_specs=in_specs, out_specs=out_specs, check_vma=False)
```

```python
import functools
import math

import jax
import jax.numpy as jnp
from jax import lax
from jax.experimental import pallas as pl
from jax.experimental.pallas import tpu as pltpu
from jax.sharding import PartitionSpec as P

HEAD = 128
BLOCK = 128
HEADS = 8
NY, NZ = 4, 8
NB = 64
HALF = NB // 2
NSLASH, NVERT = 8, 16
SLOTS = 1 + NSLASH + NVERT
D = 5120
PIECE = 512
SIDE = D // PIECE // 2
PIECES = 2 * SIDE
ROWS = 32
FEATURES = HEADS * HEAD
EXP2_SCALE = HEAD**-0.5 * math.log2(math.e)
MESH = pl.DeviceIdType.MESH
CUTS = (2, 4, 6, 8)
ROW_BLOCKS = tuple(NZ * (row + 1) for row in range(NY))
SENT = (24, 16, 22, 14)
HOPS_Z = (0, 1, 1, 2, 2)
NEG = float("-inf")


def key_slot(core, y, z):
    return core * HALF + z * NY + y


def value_slot(core, y, z):
    return core * HALF + y * NZ + z


def choose_blocks(head, me, vert_ref, count_ref, slash_ref, key_at, value_at, bias_at):
    low = jnp.where(me < 32, jnp.left_shift(jnp.int32(1), me % 32), 0)
    high = jnp.where(me < 32, 0, jnp.left_shift(jnp.int32(1), me % 32))
    count = count_ref[head]
    for c in range(1, SLOTS):
        if c <= NSLASH:
            block = me - slash_ref[head, c - 1]
            usable = block >= 0
        else:
            block = vert_ref[head, c - 1 - NSLASH]
            usable = (block <= me) & (c - 1 - NSLASH < count)
        block = jnp.where(usable, block, me)
        bit = jnp.left_shift(jnp.int32(1), block % 32)
        in_low = block < 32
        seen = (jnp.where(in_low, low, high) & bit) != 0
        kept = usable & jnp.logical_not(seen)
        add = jnp.where(kept, bit, 0)
        low = low | jnp.where(in_low, add, 0)
        high = high | jnp.where(in_low, 0, add)
        core, z, y = block % 2, (block // 2) % NZ, block // (2 * NZ)
        key_at[head, c] = key_slot(core, y, z)
        value_at[head, c] = value_slot(core, y, z)
        bias_at[head, c] = jnp.where(kept, jnp.float32(0), jnp.float32(NEG))


def slot_groups(size):
    return [list(range(c, min(c + size, SLOTS))) for c in range(0, SLOTS, size)]


def weigh_head(head, q_vm, keys_vm, key_at, bias_at, own_key, scores, weights, scale_by):
    query = q_vm[head]
    rows = lax.broadcasted_iota(jnp.int32, (BLOCK, BLOCK), 0)
    cols = lax.broadcasted_iota(jnp.int32, (BLOCK, BLOCK), 1)
    top = None
    for slots in slot_groups(2):
        keys = [keys_vm[own_key if s == 0 else key_at[head, s]] for s in slots]
        keys = keys[0] if len(keys) == 1 else jnp.concatenate(keys, axis=0)
        both = lax.dot_general(
            query, keys, (((1,), (1,)), ((), ())), preferred_element_type=jnp.float32
        )
        for n, s in enumerate(slots):
            part = both[:, n * BLOCK : (n + 1) * BLOCK]
            if s == 0:
                part = jnp.where(cols <= rows, part, NEG)
            else:
                part = part + bias_at[head, s]
            scores[:, s * BLOCK : (s + 1) * BLOCK] = part
            top = part if top is None else jnp.maximum(top, part)
    top = jnp.max(top, axis=1, keepdims=True)
    total = None
    for s in range(SLOTS):
        at = slice(s * BLOCK, (s + 1) * BLOCK)
        part = jnp.exp2((scores[:, at] - top) * EXP2_SCALE)
        weights[head, :, at] = part.astype(jnp.bfloat16)
        total = part if total is None else total + part
    total = jnp.sum(total, axis=1, keepdims=True)
    scale_by[head] = jnp.broadcast_to(1.0 / total, (BLOCK, HEAD))


def combine_head(head, half, starts, values_vm, value_at, own_value, weights, scale_by, att):
    def of_targets(ref, at):
        return jnp.concatenate([ref[head, pl.ds(start, ROWS), at] for start in starts], axis=0)

    out = None
    for slots in slot_groups(4):
        values = [values_vm[own_value if s == 0 else value_at[head, s]] for s in slots]
        values = values[0] if len(values) == 1 else jnp.concatenate(values, axis=0)
        part = of_targets(weights, slice(slots[0] * BLOCK, (slots[-1] + 1) * BLOCK))
        term = jnp.dot(part, values, preferred_element_type=jnp.float32)
        out = term if out is None else out + term
    out = out * of_targets(scale_by, slice(0, HEAD))
    att[half, :, pl.ds(pl.multiple_of(head * HEAD, HEAD), HEAD)] = out.astype(jnp.bfloat16)


def remote(src, dst, send, recv, where):
    return pltpu.make_async_remote_copy(
        src_ref=src, dst_ref=dst, send_sem=send, recv_sem=recv, device_id=where, device_id_type=MESH
    )


class Gather:
    def __init__(self, buffers, sems, sources, core, y, z, seq_at):
        self.buffers, self.sources, self.core, self.y, self.z = buffers, sources, core, y, z
        self.full_sem, self.half_sem, self.send_sem, self.twin_send, self.twin_recv = sems
        other = 1 - core
        self.up_y, self.down_y = seq_at(other, y + 1, z), seq_at(other, y - 1, z)
        self.far_y = seq_at(other, y + 2, z)
        self.along = {d: seq_at(other, y, z + d) for d in (-2, -1, 1, 2)}
        self.twin = seq_at(1 - core, y, z)

    def slot(self, kind, dy, dz):
        hops = HOPS_Z[abs(dz)] + (dy in (1, -1)) if abs(dy) < 2 else 1 + HOPS_Z[abs(dz)]
        core = self.core if hops % 2 == 0 else 1 - self.core
        at = key_slot if kind == 0 else value_slot
        return at(core, (self.y + dy + NY) % NY, (self.z + dz + NZ) % NZ)

    def send(self, kind, slot, where, half=None, source=None):
        target = self.buffers[kind].at[slot]
        source = target if source is None else source
        if half is not None:
            source = source.at[pl.ds(half * 64, 64)]
            target = target.at[pl.ds(half * 64, 64)]
        recv = (self.half_sem if half == 1 else self.full_sem).at[kind, slot % HALF]
        remote(source, target, self.send_sem.at[kind], recv, where).start()

    def to_twin(self, kind, slot, source=None):
        target = self.buffers[kind].at[slot]
        source = target if source is None else source
        send, recv = self.twin_send.at[kind], self.twin_recv.at[kind]
        remote(source, target, send, recv, self.twin).start()

    def arrived(self, kind, slot, halves=False):
        whole = self.buffers[kind].at[slot]
        if halves:
            for half, sem in ((0, self.full_sem), (1, self.half_sem)):
                piece = whole.at[pl.ds(half * 64, 64)]
                pltpu.make_async_copy(piece, piece, sem.at[kind, slot % HALF]).wait()
        else:
            pltpu.make_async_copy(whole, whole, self.full_sem.at[kind, slot % HALF]).wait()

    def beside(self, kind, slot, source=None):
        @pl.when(self.y < NY - 1)
        def _():
            self.send(kind, slot, self.up_y, source=source)

        @pl.when(self.y == 0)
        def _():
            self.send(kind, slot, self.down_y, source=source)

    def own(self, kind):
        source, slot = self.sources[kind], self.slot(kind, 0, 0)

        @pl.when(self.y < 2)
        def _():
            self.send(kind, slot, self.far_y, source=source)

        for d in (2, -2, 1, -1):
            self.send(kind, slot, self.along[d], source=source)
        self.beside(kind, slot, source)
        self.to_twin(kind, slot, source)

    def take(self, kind, dy, dz, on=(), half_on=()):
        slot = self.slot(kind, dy, dz)
        self.arrived(kind, slot, halves=dz == 4 and dy in (0, 2))
        for d in on:
            self.send(kind, slot, self.along[d])
        for d in half_on:
            self.send(kind, slot, self.along[d], half=0 if d > 0 else 1)
        if dy == 0:
            self.beside(kind, slot)
        self.to_twin(kind, slot)

    def when_far(self, *steps):
        def run():
            @pl.when(self.y >= 2)
            def _():
                for step in steps:
                    step()

        return run

    def stages(self, kind):
        take = functools.partial(self.take, kind)
        first = [functools.partial(self.own, kind)]
        near = [self.when_far(lambda: take(2, 0, (2, -2, 1, -1)))]
        near += [lambda s=s: take(0, -2 * s, (s,), (2 * s,)) for s in (1, -1)]
        near += [lambda s=s: take(0, -s) for s in (1, -1)]
        middle = [self.when_far(*(lambda s=s: take(2, -2 * s, (s,), (2 * s,)) for s in (1, -1)))]
        middle += [lambda s=s: take(0, -3 * s) for s in (1, -1)]
        middle += [lambda: take(0, 4)]
        return [first, near, middle, self.last(kind)]

    def last(self, kind):
        take = functools.partial(self.take, kind)

        def beside(*shifts):
            def run():
                @pl.when(self.y >= 1)
                def _():
                    for dz in shifts:
                        take(-1, dz)

                @pl.when(self.y == NY - 1)
                def _():
                    for dz in shifts:
                        take(1, dz)

            return run

        return [
            beside(0),
            beside(1, -1),
            self.when_far(lambda: take(2, 1), lambda: take(2, -1)),
            beside(2),
            beside(-2),
            beside(3),
            beside(-3),
            self.when_far(lambda: take(2, 3), lambda: take(2, -3)),
            beside(4),
            self.when_far(lambda: take(2, 4)),
        ]

    def by_row(self, kind, sem, blocks):
        for row, count in enumerate(blocks):

            @pl.when(self.y == row)
            def _(count=count):
                due = self.buffers[kind].at[pl.ds(0, count)]
                pltpu.make_async_copy(due, due, sem.at[kind]).wait()

    def other_half(self, kind):
        self.by_row(kind, self.twin_recv, ROW_BLOCKS)

    def sent(self):
        for kind in (0, 1):
            self.by_row(kind, self.twin_send, ROW_BLOCKS)
            self.by_row(kind, self.send_sem, SENT)


def kernel(
    vert_hbm, count_hbm, slash_hbm, q_hbm, k_hbm, v_hbm, w_hbm, out_ref,
    keys_vm, values_vm, q_vm, w_vm, scores, weights, scale_by, att, part,
    opp_in, dir_in, sum_in, sum_out,
    vert_ref, count_ref, slash_ref, key_at, value_at, bias_at,
    full_sem, half_sem, send_sem, twin_send, twin_recv, own_sem, q_sem, w_sem,
    opp_sem, dir_sem, sum_sem, first_send, second_send,
):
    me, tp = lax.axis_index("seq"), lax.axis_index("tp")
    core, z, y = me % 2, (me // 2) % NZ, me // (2 * NZ)

    def seq_at(core, y, z):
        return {"seq": ((y + NY) % NY * NZ + (z + NZ) % NZ) * 2 + core}

    right, left = {"tp": (tp + 1) % 4}, {"tp": (tp + 3) % 4}
    own_key, own_value = key_slot(core, y, z), value_slot(core, y, z)
    own_copies = [
        pltpu.make_async_copy(source, target, own_sem.at[n])
        for n, (source, target) in enumerate(
            (
                (k_hbm, keys_vm.at[own_key]),
                (v_hbm, values_vm.at[own_value]),
                (vert_hbm, vert_ref),
                (count_hbm, count_ref),
                (slash_hbm, slash_ref),
            )
        )
    ]
    moves = Gather(
        (keys_vm, values_vm), (full_sem, half_sem, send_sem, twin_send, twin_recv),
        (k_hbm, v_hbm), core, y, z, seq_at,
    )
    barrier = pltpu.get_barrier_semaphore()
    neighbours = (
        moves.up_y, moves.down_y, moves.far_y, moves.twin, right, left, *moves.along.values(),
    )
    for where in neighbours:
        pl.semaphore_signal(barrier, inc=1, device_id=where, device_id_type=MESH)
    for copy in own_copies:
        copy.start()
    pl.semaphore_wait(barrier, len(neighbours))

    keys, values = moves.stages(0), moves.stages(1)

    def do(stage):
        for handler in stage:
            handler()

    do(keys[0])
    do(values[0])
    for head in range(HEADS):
        pltpu.make_async_copy(
            q_hbm.at[:, pl.ds(head * HEAD, HEAD)], q_vm.at[head], q_sem
        ).start()
    for p in range(PIECES):
        pltpu.make_async_copy(
            w_hbm.at[:, pl.ds(p * PIECE, PIECE)], w_vm.at[p], w_sem.at[p]
        ).start()
    for copy in own_copies:
        copy.wait()

    @pl.loop(0, HEADS)
    def _(head):
        choose_blocks(head, me, vert_ref, count_ref, slash_ref, key_at, value_at, bias_at)

    for stage in (keys[1], values[1], keys[2], values[2], keys[3]):
        do(stage)
    pltpu.make_async_copy(q_vm, q_vm, q_sem).wait()
    moves.other_half(0)

    def weigh(head, n):
        weigh_head(
            head, q_vm, keys_vm, key_at, bias_at, own_key, scores.at[n], weights, scale_by
        )

    ends = values[3]
    cuts = [0] + [len(ends) * c // 8 for c in CUTS] + [len(ends)]
    for n in range(HEADS // 2):
        do(ends[cuts[n] : cuts[n + 1]])
        weigh(2 * n, 0)
        weigh(2 * n + 1, 1)
    do(ends[cuts[HEADS // 2] :])
    moves.other_half(1)

    starts = [
        [pl.multiple_of((tp + ahead) % 4 * ROWS, ROWS) for ahead in pair]
        for pair in ((2, 1), (3, 0))
    ]
    first, second = pl.ds(0, ROWS), pl.ds(ROWS, ROWS)

    def project(half, p):
        part[half, p] = jnp.dot(
            att[half], w_vm[p], preferred_element_type=jnp.float32
        ).astype(jnp.bfloat16)

    def combine(half):
        @pl.loop(0, HEADS // 2)
        def _(pair):
            for n in range(2):
                combine_head(
                    pair * 2 + n, half, starts[half], values_vm, value_at, own_value,
                    weights, scale_by, att,
                )

    def send_direct(half, rows, p, where):
        remote(part.at[half, p, rows], dir_in.at[p], first_send, dir_sem.at[p], where).start()

    combine(0)

    @pl.loop(0, SIDE)
    def _(j):
        for p, ahead in ((j, right), (j + SIDE, left)):
            pltpu.make_async_copy(w_vm.at[p], w_vm.at[p], w_sem.at[p]).wait()
            project(0, p)
            remote(part.at[0, p, first], opp_in.at[p], first_send, opp_sem.at[p], ahead).start()
        send_direct(0, second, j + SIDE, right)

    combine(1)

    @pl.loop(0, SIDE)
    def _(j):
        project(1, j)
        send_direct(1, first, j, left)
        project(1, j + SIDE)

    @pl.loop(0, SIDE)
    def _(j):
        for p, ahead, half, rows in ((j, right, 0, second), (j + SIDE, left, 1, first)):
            pltpu.make_async_copy(opp_in.at[p], opp_in.at[p], opp_sem.at[p]).wait()
            summed = opp_in[p].astype(jnp.float32) + part[half, p, rows].astype(jnp.float32)
            sum_out[p] = summed.astype(jnp.bfloat16)
            remote(sum_out.at[p], sum_in.at[p], second_send, sum_sem.at[p], ahead).start()

    for j in range(SIDE):
        for p in (j, j + SIDE):
            pltpu.make_async_copy(dir_in.at[p], dir_in.at[p], dir_sem.at[p]).wait()
            pltpu.make_async_copy(sum_in.at[p], sum_in.at[p], sum_sem.at[p]).wait()
            whole = (
                part[1, p, second].astype(jnp.float32)
                + dir_in[p].astype(jnp.float32)
                + sum_in[p].astype(jnp.float32)
            )
            out_ref[:, p * PIECE : (p + 1) * PIECE] = whole.astype(jnp.bfloat16)
    pltpu.make_async_copy(part.at[0], part.at[0], first_send).wait()
    pltpu.make_async_copy(sum_out, sum_out, second_send).wait()
    moves.sent()


def body(queries, key_vectors, value_vectors, vertical, vertical_count, slash_offsets, out_weight):
    anywhere = pl.BlockSpec(memory_space=pl.ANY)
    bf16, dma = jnp.bfloat16, pltpu.SemaphoreType.DMA
    inputs = (
        vertical, vertical_count, slash_offsets, queries, key_vectors, value_vectors, out_weight
    )
    return pl.pallas_call(
        kernel,
        out_shape=jax.ShapeDtypeStruct((ROWS, D), bf16),
        in_specs=[anywhere] * 7,
        out_specs=pl.BlockSpec(memory_space=pltpu.VMEM),
        scratch_shapes=[
            pltpu.VMEM((NB, BLOCK, HEAD), bf16),
            pltpu.VMEM((NB, BLOCK, HEAD), bf16),
            pltpu.VMEM((HEADS, BLOCK, HEAD), bf16),
            pltpu.VMEM((PIECES, FEATURES, PIECE), bf16),
            pltpu.VMEM((2, BLOCK, SLOTS * BLOCK), jnp.float32),
            pltpu.VMEM((HEADS, BLOCK, SLOTS * BLOCK), bf16),
            pltpu.VMEM((HEADS, BLOCK, HEAD), jnp.float32),
            pltpu.VMEM((2, 2 * ROWS, FEATURES), bf16),
            pltpu.VMEM((2, PIECES, 2 * ROWS, PIECE), bf16),
            pltpu.VMEM((PIECES, ROWS, PIECE), bf16),
            pltpu.VMEM((PIECES, ROWS, PIECE), bf16),
            pltpu.VMEM((PIECES, ROWS, PIECE), bf16),
            pltpu.VMEM((PIECES, ROWS, PIECE), bf16),
            pltpu.SMEM((HEADS, NVERT), jnp.int32),
            pltpu.SMEM((HEADS,), jnp.int32),
            pltpu.SMEM((HEADS, NSLASH), jnp.int32),
            pltpu.SMEM((HEADS, 32), jnp.int32),
            pltpu.SMEM((HEADS, 32), jnp.int32),
            pltpu.SMEM((HEADS, 32), jnp.float32),
            dma((2, HALF)),
            dma((2, HALF)),
            dma((2,)),
            dma((2,)),
            dma((2,)),
            dma((5,)),
            dma,
            dma((PIECES,)),
            dma((PIECES,)),
            dma((PIECES,)),
            dma((PIECES,)),
            dma,
            dma,
        ],
        compiler_params=pltpu.CompilerParams(
            collective_id=0, has_side_effects=True, vmem_limit_bytes=48 * 1024 * 1024
        ),
        cost_estimate=pl.CostEstimate(
            flops=3_200_000_000, bytes_accessed=16_000_000, transcendentals=3_300_000
        ),
        name="attend_project",
    )(*[pltpu.with_memory_space_constraint(a, pltpu.HBM) for a in inputs])


def solution(mesh):
    in_specs = (
        P("seq", "tp"),
        P("seq", "tp"),
        P("seq", "tp"),
        P("tp", None),
        P("tp"),
        P("tp", None),
        P("tp", None),
    )
    out_specs = P(("seq", "tp"), None)
    return jax.shard_map(body, mesh=mesh, in_specs=in_specs, out_specs=out_specs, check_vma=False)
```
